256 devices in a mesh: gx: 64 (over z, y, x_lo), gy: 4 (over x_hi, core).
Axes of the slice: x: 4 (x_hi: 2, x_lo: 2; x = x_hi * 2 + x_lo), y: 4, z: 8, core: 2. Of those that a mesh axis runs over, the one named last changes fastest.
Arguments:
- points: bfloat16 [64, 4, 1024, 192], P('gx', 'gy'), may hold values from -6 to 6
- gain: float32 [192], replicated, may hold values from 0.1 to 1.9
- w_query: bfloat16 [192, 192], replicated
- w_key: bfloat16 [192, 192], replicated
- w_value: bfloat16 [192, 192], replicated, may hold values from -0.4375 to 0.4375
- w_out: bfloat16 [192, 192], replicated, may hold values from -0.4375 to 0.4375
- lengths: int32 [64, 4, 24], P('gx', 'gy'), may hold values from 1 to 64, 1024 in all within a row
- picks: int32 [64, 4, 24, 64], P('gx', 'gy'), may hold values from 0 to 575, as said below
- cotangent: bfloat16 [64, 4, 1024, 192], P('gx', 'gy'), may hold values from -8 to 8
Outputs:
- layer_out: bfloat16 [64, 4, 1024, 192], P('gx', 'gy')
- feature_gradient: float32 [64, 4, 1024, 192], P('gx', 'gy')
- grad_weights: float32 [4, 192, 192], replicated
- gain_gradient: float32 [192], replicated
The draws below stay inside these ranges and needn't reach their ends.
Inputs may be any that keep to these rules, and one draw needn't show every extreme that they name: Each block's window lengths sum to 1024; points are stored window after window. `picks`: a pick p names row p % 64 of neighbourhood block p // 64, never a block off the grid.
All inputs are finite; a program needn't handle non-finite values.
Results may differ from the reference program's by a relative error of at most 0.012.
The reference program's roundings to bfloat16 on the way count: a program that leaves them out, or rounds other values in their place, can miss the bound.
Values may be sent and summed in bfloat16 or wider, within the bound.
No kernel may reach another device: no remote copies, remote signals or barrier semaphores. Data moves between devices by JAX's collectives and lax.ppermute only.
A program may use at most 64 MiB of HBM per device.

```python
import math
import jax
import jax.numpy as jnp
import numpy as np
from jax import lax

C = 192
H = 6
P_DEV = 1024
WIN = 64
S_PICK = 64
W_DEV = 24
SAMP = 64
POINTS = 262144
N_GX = 64
N_GY = 4


def draw_w_query(key, part):
    key = jax.random.fold_in(key, 11)
    return (jax.random.normal(key, (C, C), jnp.float32) * C ** (-0.5)).astype(jnp.bfloat16)


def draw_w_key(key, part):
    key = jax.random.fold_in(key, 17)
    own = jax.random.normal(key, (C, C), jnp.float32)
    return (own * C ** (-0.5)).astype(jnp.bfloat16)


def draw_picks(key, part):
    key = jax.random.fold_in(key, 23)
    first, second = jax.random.split(key)
    shape = (N_GX, N_GY, W_DEV, S_PICK)
    block = jax.random.randint(first, shape, 0, 9, dtype=jnp.int32)
    offset = jax.random.randint(second, shape, 0, SAMP, dtype=jnp.int32)
    row = lax.broadcasted_iota(jnp.int32, shape, 0) + block // 3 - 1
    col = lax.broadcasted_iota(jnp.int32, shape, 1) + block % 3 - 1
    inside = (row >= 0) & (row < N_GX) & (col >= 0) & (col < N_GY)
    block = jnp.where(inside, block, 4)
    return (block * SAMP + offset).astype(jnp.int32)


def with_spikes(drawn, rng, source, target, parts, factor):
    owner, partner = [(jnp.arange(drawn.shape[dim]) // (drawn.shape[dim] // parts)).reshape([-1 if axis == dim else 1 for axis in range(drawn.ndim)]) for dim in (source, target)]
    chosen = jax.random.permutation(rng, parts)[partner]
    strong = (owner == chosen) | (owner == (partner + parts // 2) % parts)
    return jnp.where(strong, factor * drawn, drawn)


def levels(own_key, shape, cuts, least, largest):
    level, own = 1.0, jax.random.fold_in(own_key, 6)
    for dim, blocks in cuts:
        draws = jnp.exp(jax.random.uniform(jax.random.fold_in(own, dim), (blocks,), jnp.float32, least / len(cuts), largest / len(cuts)))
        level = level * jnp.repeat(draws, shape[dim] // blocks).reshape([-1 if axis == dim else 1 for axis in range(len(shape))])
    return level


def length_profile(count, total, most, skew):
    loads = [(1 << 20) // math.isqrt(standing ** skew) + 1 for standing in range(2, count + 1)]
    spare, holding = total - most - (count - 1), [1] * (count - 1)
    while spare > 0:
        movable = [i for i in range(count - 1) if holding[i] < most]
        whole, budget = sum([loads[i] for i in movable]), spare
        for i in movable:
            more = min(most - holding[i], max(1, budget * loads[i] // whole), spare)
            holding[i] = holding[i] + more
            spare = spare - more
    return np.array([most] + holding)


def uneven_parts(rng, number_of, total, most, lean):
    if number_of == 2:
        one = jax.random.randint(rng, (), max(1, total - most), min(most, total - 1) + 1)
        return jnp.stack([one, total - one])
    sizes = jnp.asarray(length_profile(number_of, total, most, lean), jnp.int32)
    twos = (number_of - 1) // 2
    source_of, taker = sizes[1:1 + 2 * twos:2], sizes[2:2 + 2 * twos:2]
    room = jnp.minimum(source_of - 1, most - taker)
    moved = jax.random.randint(jax.random.fold_in(rng, 1), (twos,), 0, 1 << 20) % (room + 1)
    sizes = sizes.at[1:1 + 2 * twos:2].set(source_of - moved).at[2:2 + 2 * twos:2].set(taker + moved)
    return sizes[jax.random.permutation(jax.random.fold_in(rng, 2), number_of)]


def normal_values(stream_key, extent, scale, limit, cuts=(), kind=jnp.bfloat16):
    result = scale * jax.random.normal(stream_key, extent, jnp.float32)
    if cuts:
        result = result * levels(stream_key, extent, cuts, -0.22, 0.18)
    return jnp.clip(result, -limit, limit).astype(kind)


def noise_with(key, dims, scale, most, shards, heavy, kind=jnp.bfloat16):
    drawn = scale * jax.random.normal(key, dims, jnp.float32)
    if shards:
        drawn = drawn * levels(key, dims, shards, -0.22, 0.18)
    return jnp.clip(with_spikes(drawn, jax.random.fold_in(key, 3), *heavy), -most, most).astype(kind)


def setup_inputs(seed: int = 0) -> dict:
    streams_of = jax.random.split(jax.random.key(seed), 10)
    points = normal_values(streams_of[0], (N_GX, N_GY, P_DEV, C), 1.0, 6.0, ((0, 64), (1, 4)))
    gain = jnp.clip(1.0 + 0.18 * jax.random.normal(streams_of[1], (C,), jnp.float32), 0.1, 1.9)
    w_query = draw_w_query(jax.random.fold_in(streams_of[9], 71), 0)
    w_key = draw_w_key(jax.random.fold_in(streams_of[9], 71), 0)
    w_value = normal_values(streams_of[4], (C, C), C ** -0.5, 0.4375)
    w_out = normal_values(streams_of[5], (C, C), C ** -0.5, 0.4375)
    lengths = jax.vmap(lambda own: uneven_parts(own, W_DEV, P_DEV, WIN, 2))(jax.random.split(streams_of[6], N_GX * N_GY)).reshape((N_GX, N_GY, W_DEV)).astype(jnp.int32)
    picks = draw_picks(jax.random.fold_in(streams_of[9], 71), 0)
    cotangent = noise_with(streams_of[8], (N_GX, N_GY, P_DEV, C), 1.0, 8.0, ((0, 64), (1, 4)), (0, 3, 64, 4.0))
    return dict(points=points, gain=gain, w_query=w_query, w_key=w_key, w_value=w_value, w_out=w_out, lengths=lengths, picks=picks, cotangent=cotangent)


window_groups = 6

def layer_statistics(features_f32):
    feature_mean = lax.optimization_barrier(jnp.mean(features_f32, axis=-1, keepdims=True))
    centred = features_f32 - feature_mean
    variance = lax.optimization_barrier(jnp.mean(centred * centred, axis=-1, keepdims=True))
    inverse_deviation = lax.rsqrt(variance + 1e-05)
    return (centred * inverse_deviation, inverse_deviation)

def attend_core(query_win, keys, values, live):
    groups, slots, width = query_win.shape
    count = keys.shape[1]
    heads = H
    depth = width // heads
    qh = query_win.astype(jnp.float32).reshape(groups, slots, heads, depth)
    kh = keys.astype(jnp.float32).reshape(groups, count, heads, depth)
    vh = values.astype(jnp.float32).reshape(groups, count, heads, depth)
    scores = jnp.einsum('gqhd,gkhd->ghqk', qh, kh) * depth ** (-0.5)
    scores = jnp.where(live[:, None, None, :], scores, -1e+30)
    top = lax.optimization_barrier(jnp.max(scores, axis=-1, keepdims=True))
    weights = jnp.exp(scores - top)
    probs = (weights / lax.optimization_barrier(jnp.sum(weights, axis=-1, keepdims=True))).astype(jnp.bfloat16)
    out = jnp.einsum('ghqk,gkhd->gqhd', probs.astype(jnp.float32), vh)
    return out.reshape(groups, slots, width).astype(jnp.bfloat16)

def attend_device(query, key, value, lengths, picks, nearby):
    count, width = query.shape
    windows = lengths.shape[0]
    offsets = (jnp.cumsum(lengths) - lengths).astype(jnp.int32)
    slots = jnp.arange(WIN, dtype=jnp.int32)
    live_dense = slots[None, :] < lengths[:, None]
    rows = jnp.where(live_dense, offsets[:, None] + slots[None, :], 0)
    query_win = query[rows]
    key_win = key[rows]
    value_win = value[rows]
    chosen = nearby[picks].astype(jnp.bfloat16)
    keys = jnp.concatenate([key_win, chosen[:, :, :width]], axis=1)
    values = jnp.concatenate([value_win, chosen[:, :, width:]], axis=1)
    live = jnp.concatenate([live_dense, jnp.ones(picks.shape, dtype=bool)], axis=1)
    per_group = windows // window_groups

    def split(arr):
        return arr.reshape((window_groups, per_group) + arr.shape[1:])
    core = jax.checkpoint(lambda items: attend_core(*items))
    out = lax.map(core, (split(query_win), split(keys), split(values), split(live)))
    flat_out = out.reshape(windows * WIN, width)
    ends = offsets + lengths
    position = jnp.arange(count, dtype=jnp.int32)
    before = (ends[None, :] <= position[:, None]).astype(jnp.int32)
    target = position + lax.optimization_barrier(jnp.sum(before * (WIN - lengths)[None, :], axis=1)).astype(jnp.int32)
    return flat_out[target]

def reference(points, gain, w_query, w_key, w_value, w_out, lengths, picks, cotangent):
    features_f32 = points.astype(jnp.float32)
    standardized_features, inverse_deviation = layer_statistics(features_f32)
    normalized_features = (standardized_features * gain).astype(jnp.bfloat16)
    query = jnp.dot(normalized_features, w_query, preferred_element_type=jnp.float32).astype(jnp.bfloat16)
    key = jnp.dot(normalized_features, w_key, preferred_element_type=jnp.float32).astype(jnp.bfloat16)
    value = jnp.dot(normalized_features, w_value, preferred_element_type=jnp.float32).astype(jnp.bfloat16)
    both = jnp.concatenate([key, value], axis=-1)
    sample = both.reshape(N_GX, N_GY, SAMP, 16, 2 * C)[:, :, :, 0].astype(jnp.float32)
    padded = jnp.pad(sample, ((1, 1), (1, 1), (0, 0), (0, 0)))
    d_attended = jnp.dot(cotangent, w_out.T, preferred_element_type=jnp.float32).astype(jnp.bfloat16)
    blocks = N_GX * N_GY

    def one_block(items):
        index, q_b, k_b, v_b, len_b, pick_b, d_b = items
        row = (index // N_GY).astype(jnp.int32)
        col = (index % N_GY).astype(jnp.int32)
        zero = jnp.zeros((), jnp.int32)
        nearby = lax.dynamic_slice(padded, (row, col, zero, zero), (3, 3, SAMP, 2 * C)).reshape(9 * SAMP, 2 * C)

        def local(q_in, k_in, v_in, n_in):
            return attend_device(q_in, k_in, v_in, len_b, pick_b, n_in)
        out, pull = jax.vjp(local, q_b, k_b, v_b, nearby)
        dq, dk, dv, dn = pull(d_b)
        return (out, dq, dk, dv, dn.reshape(3, 3, SAMP, 2 * C))
    flat = lambda arr: arr.reshape((blocks,) + arr.shape[2:])
    attended, d_query, d_key, d_value, d_near = lax.map(one_block, (jnp.arange(blocks, dtype=jnp.int32), flat(query), flat(key), flat(value), flat(lengths), flat(picks), flat(d_attended)))
    shape4 = (N_GX, N_GY, P_DEV, C)
    attended = attended.reshape(shape4)
    d_query = d_query.reshape(shape4)
    d_key = d_key.reshape(shape4)
    d_value = d_value.reshape(shape4)
    d_near = d_near.reshape(N_GX, N_GY, 3, 3, SAMP, 2 * C)
    gathered = jnp.zeros((N_GX + 2, N_GY + 2, SAMP, 2 * C), jnp.float32)
    for i in range(3):
        for j in range(3):
            gathered = gathered.at[i:i + N_GX, j:j + N_GY].add(d_near[:, :, i, j])
    returned = gathered[1:-1, 1:-1].astype(jnp.bfloat16)
    d_key = d_key.reshape(N_GX, N_GY, SAMP, 16, C).at[:, :, :, 0].add(returned[..., :C]).reshape(shape4)
    d_value = d_value.reshape(N_GX, N_GY, SAMP, 16, C).at[:, :, :, 0].add(returned[..., C:]).reshape(shape4)
    layer_out = (features_f32 + jnp.dot(attended, w_out, preferred_element_type=jnp.float32)).astype(jnp.bfloat16)
    normalized_gradient = jnp.dot(d_query, w_query.T, preferred_element_type=jnp.float32)
    normalized_gradient = normalized_gradient + jnp.dot(d_key, w_key.T, preferred_element_type=jnp.float32)
    normalized_gradient = normalized_gradient + jnp.dot(d_value, w_value.T, preferred_element_type=jnp.float32)
    centered_gradient = normalized_gradient * gain
    feature_gradient = inverse_deviation * (centered_gradient - lax.optimization_barrier(jnp.mean(centered_gradient, axis=-1, keepdims=True)) - standardized_features * lax.optimization_barrier(jnp.mean(centered_gradient * standardized_features, axis=-1, keepdims=True))) + cotangent.astype(jnp.float32)
    scale_factor = POINTS ** (-0.5)
    row_pairs2 = lambda arr: arr.reshape(-1, C)
    grad_weights = jnp.stack([jnp.dot(row_pairs2(normalized_features).T, row_pairs2(d_query), preferred_element_type=jnp.float32), jnp.dot(row_pairs2(normalized_features).T, row_pairs2(d_key), preferred_element_type=jnp.float32), jnp.dot(row_pairs2(normalized_features).T, row_pairs2(d_value), preferred_element_type=jnp.float32), jnp.dot(row_pairs2(attended).T, row_pairs2(cotangent), preferred_element_type=jnp.float32)]) * scale_factor
    gain_gradient = lax.optimization_barrier(jnp.sum(row_pairs2(normalized_gradient * standardized_features), axis=0)) * scale_factor
    return (layer_out, feature_gradient, grad_weights, gain_gradient)
```

```python
import jax
import jax.numpy as jnp
from jax import lax
from jax.experimental import pallas as pl
from jax.experimental.pallas import tpu as pltpu
from jax.sharding import Mesh, PartitionSpec as P

C = 192
H = 6
DEPTH = 32
PTS = 1024
WIN = 64
NWIN = 24
SAMP = 64
NEAR = 9 * SAMP
PAD = PTS + WIN
ROWS = 1280
HALF = ROWS // 2
GX = ("z", "y", "xl")
GY = ("xh", "c")
XY = ("y", "xl", "xh")
SCALE = DEPTH ** (-0.5)
LOG2E = 1.4426950408889634
F32 = jnp.float32
BF16 = jnp.bfloat16
VMEM = pl.BlockSpec(memory_space=pltpu.VMEM)
SMEM = pl.BlockSpec(memory_space=pltpu.SMEM)


def nn(a, b):
    return lax.dot_general(a, b, (((1,), (0,)), ((), ())), preferred_element_type=F32)


def nt(a, b):
    return lax.dot_general(a, b, (((1,), (1,)), ((), ())), preferred_element_type=F32)


def tn(a, b):
    return lax.dot_general(a, b, (((0,), (0,)), ((), ())), preferred_element_type=F32)


def standardize(x):
    mean = jnp.sum(x, axis=-1, keepdims=True) * (1.0 / C)
    centred = x - mean
    variance = jnp.sum(centred * centred, axis=-1, keepdims=True) * (1.0 / C)
    inverse = lax.rsqrt(variance + 1e-05)
    return centred * inverse, inverse


def pre_kernel(points, gain, w_in, w_back, cot, picks_row, picks_col,
               qa, ka, va, da, kvb, qdb, xhat, normed_t, onehot, onehot_t):
    chunk = 128

    def project(i, _):
        rows = pl.ds(pl.multiple_of(i * chunk, chunk), chunk)
        hat, _inv = standardize(points[rows, :].astype(F32))
        xhat[rows, :] = hat
        normed = (hat * gain[...]).astype(BF16)
        wide = nn(normed, w_in[...])
        back = nt(cot[rows, :], w_back[...])
        both = (wide[:, 512:], back[:, 128:])
        for ref, x in ((qa, wide[:, :128]), (ka, wide[:, 128:256]), (va, wide[:, 256:384]),
                       (kvb, wide[:, 384:512]), (da, back[:, :128]), (qdb, both[0] + both[1])):
            ref[rows, :] = x.astype(BF16).astype(F32)
        normed_t[:, rows] = normed.astype(F32).T.astype(BF16)
        return 0

    lax.fori_loop(0, PTS // chunk, project, 0)
    zeros = jnp.zeros((WIN, 128), F32)
    for ref in (qa, ka, va, da, kvb, qdb):
        ref[PTS:, :] = zeros

    def rows_hot(i, _):
        rows = pl.ds(pl.multiple_of(i * WIN, WIN), WIN)
        ids = lax.broadcasted_iota(jnp.int32, (WIN, NEAR), 1)
        onehot[rows, :] = jnp.where(picks_col[rows, :] == ids, 1.0, 0.0).astype(BF16)
        return 0

    lax.fori_loop(0, NWIN, rows_hot, 0)

    def columns_hot(i, _):
        rows = pl.ds(pl.multiple_of(i * SAMP, SAMP), SAMP)
        ids = lax.broadcasted_iota(jnp.int32, (SAMP, NWIN * WIN), 0) + i * SAMP
        onehot_t[rows, :] = jnp.where(picks_row[...] == ids, 1.0, 0.0).astype(BF16)
        return 0

    lax.fori_loop(0, 9, columns_hot, 0)


def attend_kernel(lengths, place, near_points, gain, w_in, cot, qa, ka, va, da, kvb, qdb, xhat,
                  normed_t, onehot, onehot_t,
                  keep, send, d_near, grads,
                  near_hat, near_normed, near_kv, pick, d_pick,
                  oa_s, dqa_s, dka_s, dva_s, dkvb_s, dqob_s, packed):
    hat, _inv = standardize(near_points[...].astype(F32))
    near_hat[...] = hat
    normed = (hat * gain[...]).astype(BF16)
    near_normed[...] = normed
    near_kv[...] = nn(normed, w_in[:, 128:512]).astype(BF16)

    def choose(i, _):
        rows = pl.ds(pl.multiple_of(i * 256, 256), 256)
        pick[rows, :] = nn(onehot[rows, :], near_kv[...]).astype(BF16)
        return 0

    lax.fori_loop(0, NWIN * WIN // 256, choose, 0)

    row_head = lax.broadcasted_iota(jnp.int32, (4 * WIN, 128), 0) // WIN
    lane_head = lax.broadcasted_iota(jnp.int32, (4 * WIN, 128), 1) // DEPTH
    mask = jnp.where(row_head == lane_head, 1.0, 0.0)
    mask16 = mask.astype(BF16)
    key_id = lax.broadcasted_iota(jnp.int32, (1, 128), 1)
    slot = lax.broadcasted_iota(jnp.int32, (WIN, 1), 0)
    half_scale = jnp.where(key_id < 64, SCALE, 1.0)

    def per_head(x):
        return jnp.concatenate([x] * 4, axis=0) * mask16

    def merge(x):
        x = x * mask
        return (x[:WIN] + x[WIN:2 * WIN]) + (x[2 * WIN:3 * WIN] + x[3 * WIN:])

    def softmax(scores, bias):
        scores = scores + bias
        top = jnp.max(scores, axis=-1, keepdims=True)
        weights = jnp.exp2((scores - top) * (SCALE * LOG2E))
        return weights * (1.0 / jnp.sum(weights, axis=-1, keepdims=True))

    def score_gradient(probs, d_probs):
        d_probs = d_probs.astype(BF16).astype(F32)
        inner = jnp.sum(d_probs * probs, axis=-1, keepdims=True)
        return (probs * (d_probs - inner)).astype(BF16)

    def window(w, offset):
        count = lengths[w]
        rows = pl.ds(offset, WIN)
        own = pl.ds(pl.multiple_of(w * WIN, WIN), WIN)
        bias = jnp.where((key_id >= count) & (key_id < WIN), -1e30, 0.0)
        alive = slot < count
        keys = jnp.concatenate([ka[rows, :].astype(BF16), pick[own, 0:128]], axis=0)
        values = jnp.concatenate([va[rows, :].astype(BF16), pick[own, 128:256]], axis=0)
        both = jnp.concatenate([kvb[rows, :].astype(BF16), pick[own, 256:384]], axis=0)
        qe = per_head(qa[rows, :].astype(BF16))
        de = per_head(jnp.where(alive, da[rows, :], 0.0).astype(BF16))
        qde = per_head(jnp.where(alive, qdb[rows, :], 0.0).astype(BF16))
        probs = softmax(nt(qe, keys), bias)
        probs16 = probs.astype(BF16)
        d_scores = score_gradient(probs, nt(de, values))
        mixed = nt(qde, both)
        probs_b = softmax(mixed[:128], bias)
        d_scores_b = score_gradient(probs_b, mixed[128:])
        back = jnp.concatenate([d_scores_b, probs_b.astype(BF16)], axis=0)
        oa_s[rows, :] = merge(nn(probs16, values))
        dqa_s[rows, :] = merge(nn(d_scores, keys)) * SCALE
        dqob_s[rows, :] = merge(nn(back, both)) * half_scale
        d_keys = tn(d_scores, qe) * SCALE
        d_values = tn(probs16, de)
        d_both = tn(back, qde) * half_scale
        dka_s[rows, :] = d_keys[:WIN]
        dva_s[rows, :] = d_values[:WIN]
        dkvb_s[rows, :] = d_both[:WIN]
        d_pick[own, 0:128] = d_keys[WIN:].astype(BF16)
        d_pick[own, 128:256] = d_values[WIN:].astype(BF16)
        d_pick[own, 256:384] = d_both[WIN:].astype(BF16)
        return offset + count

    lax.fori_loop(0, NWIN, window, jnp.int32(0))

    for i, ref in enumerate((dqa_s, dka_s, dva_s, dkvb_s, dqob_s, oa_s)):
        grads[:, 128 * i:128 * (i + 1)] = ref[:PTS, :].astype(BF16)
    near = nn(onehot_t[...], d_pick[...])
    near16 = near.astype(BF16)
    d_near[...] = near16
    rest = (near - near16.astype(F32)).astype(BF16)
    wide = nn(normed_t[...], grads[:, 0:640])
    near_wide = tn(near_normed[...], near16) + tn(near_normed[...], rest)
    out_a = tn(grads[:, 640:768], cot[...])
    out_b = tn(grads[:, 512:640], cot[...])
    packed[0:192, :] = wide[:, 0:128]
    packed[192:384, :] = wide[:, 128:256] + near_wide[:, 0:128]
    packed[384:576, :] = wide[:, 256:384] + near_wide[:, 128:256]
    packed[576:704, :] = out_a[:, 0:128]
    packed[704:768, :] = out_b[64:128, 0:128]
    packed[768:960, :] = wide[:, 384:512] + near_wide[:, 256:384]
    tail = jnp.concatenate([out_a[:, 128:192], out_b[64:128, 128:192]], axis=0)
    packed[960:1152, :] = jnp.concatenate([wide[:, 512:576], tail], axis=1)

    def gain_part(i, total):
        rows = pl.ds(pl.multiple_of(i * 128, 128), 128)
        d = nt(grads[rows, 0:640], w_in[...])
        return total + jnp.sum((d * xhat[rows, :]).reshape(16, 8, C), axis=0)

    total = lax.fori_loop(0, PTS // 128, gain_part, jnp.zeros((8, C), F32))
    d = nt(near16, w_in[:, 128:512]) + nt(rest, w_in[:, 128:512])
    total = total + jnp.sum((d * near_hat[...]).reshape(NEAR // 8, 8, C), axis=0)
    gain_sum = jnp.sum(total, axis=0, keepdims=True)
    packed[1152:, :] = jnp.zeros((ROWS - 1152, 128), F32)
    packed[1152:1153, :] = gain_sum[:, :128]
    packed[1153:1154, 0:64] = gain_sum[:, 128:]
    mine = place[0]
    keep[...] = packed[pl.ds(pl.multiple_of(mine * HALF, HALF), HALF), :]
    send[...] = packed[pl.ds(pl.multiple_of((1 - mine) * HALF, HALF), HALF), :]


def finish_kernel(points, gain, w_in, w_back, cot, grads, returned, layer_out, feature_gradient):
    chunk = 128

    def part(i, _):
        rows = pl.ds(pl.multiple_of(i * chunk, chunk), chunk)
        x = points[rows, :].astype(F32)
        hat, inverse = standardize(x)
        row = lax.broadcasted_iota(jnp.int32, (chunk, SAMP), 0) + i * chunk
        column = lax.broadcasted_iota(jnp.int32, (chunk, SAMP), 1)
        spread = jnp.where(row == column * 16, 1.0, 0.0).astype(BF16)
        total = (grads[rows, 128:512].astype(F32) + nn(spread, returned[...])).astype(BF16)
        d = nt(grads[rows, 0:128], w_in[:, 0:128]) + nt(total, w_in[:, 128:512])
        d = d + nt(grads[rows, 512:640], w_in[:, 512:640])
        d = d * gain[...]
        mean = jnp.sum(d, axis=-1, keepdims=True) * (1.0 / C)
        along = jnp.sum(d * hat, axis=-1, keepdims=True) * (1.0 / C)
        feature_gradient[rows, :] = inverse * (d - mean - hat * along) + cot[rows, :].astype(F32)
        mixed = nn(grads[rows, 640:768], w_back[0:128, :]) + nn(grads[rows, 512:640], w_back[128:256, :])
        layer_out[rows, :] = (x + mixed).astype(BF16)
        return 0

    lax.fori_loop(0, PTS // chunk, part, 0)


def unpack_kernel(place, own, other, weights, gain_gradient, packed):
    mine = place[0]
    factor = (PTS * 256) ** (-0.5)
    packed[pl.ds(pl.multiple_of(mine * HALF, HALF), HALF), :] = own[...] * factor
    packed[pl.ds(pl.multiple_of((1 - mine) * HALF, HALF), HALF), :] = other[...] * factor
    for i, (tail, side) in enumerate(((960, 0), (768, 0), (768, 64), (960, 64))):
        weights[i, :, 0:128] = packed[192 * i:192 * (i + 1), :]
        weights[i, :, 128:C] = packed[tail:tail + 192, side:side + 64]
    gain_gradient[:, 0:128] = packed[1152:1153, :]
    gain_gradient[:, 128:C] = packed[1153:1154, 0:64]


def call(kernel, outs, specs, scratch=(), limit=48):
    return pl.pallas_call(
        kernel,
        out_shape=[jax.ShapeDtypeStruct(s, t) for s, t in outs],
        in_specs=specs,
        out_specs=[VMEM] * len(outs),
        scratch_shapes=[pltpu.VMEM(s, t) for s, t in scratch],
        compiler_params=pltpu.CompilerParams(vmem_limit_bytes=limit * 1024 * 1024),
    )


def moved(block, axes, count, distance):
    route = [(i - distance, i) for i in range(count) if 0 <= i - distance < count]
    return lax.ppermute(block, axes, route)


def extended(rows, axes, count):
    return jnp.concatenate([moved(rows, axes, count, 1), rows, moved(rows, axes, count, -1)], axis=0)


def reduced(keep, send):
    pair = [(0, 1), (1, 0)]
    x = keep + lax.ppermute(send, "c", pair)
    x = lax.all_to_all(x.reshape(16, HALF // 16, 128), XY, 0, 0, tiled=True).sum(0)
    x = jnp.broadcast_to(x[None], (8,) + x.shape)
    x = lax.all_to_all(x, "z", 0, 0, tiled=True).sum(0)
    x = jnp.broadcast_to(x[None], (16,) + x.shape)
    x = lax.all_to_all(x, XY, 0, 0, tiled=True).reshape(HALF, 128)
    return x, lax.ppermute(x, "c", pair)


def body(points, gain, w_query, w_key, w_value, w_out, lengths, picks, cotangent):
    points = points[0, 0]
    cotangent = cotangent[0, 0]
    lengths = lengths.reshape(NWIN)
    gain = gain.reshape(1, C)
    place = lax.axis_index("c").astype(jnp.int32).reshape(1)
    sample = points.reshape(SAMP, 16, C)[:, 0]
    across = extended(sample, GY, 4)
    near = extended(across.reshape(3 * SAMP, C), GX, 64)
    empty = jnp.zeros((C, 64), BF16)
    w_in = jnp.concatenate([w_query[:, :128], w_key[:, :128], w_value[:, :128], w_key[:, 128:],
                            w_value[:, 128:], w_query[:, 128:], empty], axis=1)
    w_back = jnp.concatenate([w_out[:128], empty.T, w_out[128:]], axis=0)
    big = (PAD, 128)
    qa, ka, va, da, kvb, qdb, xhat, normed_t, onehot, onehot_t = call(
        pre_kernel,
        [(big, F32)] * 6
        + [((PTS, C), F32), ((C, PTS), BF16), ((NWIN * WIN, NEAR), BF16), ((NEAR, NWIN * WIN), BF16)],
        [VMEM] * 7,
    )(points, gain, w_in, w_back, cotangent,
      picks.reshape(1, NWIN * WIN), picks.reshape(NWIN * WIN, 1))
    keep, send, d_near, grads = call(
        attend_kernel,
        [((HALF, 128), F32)] * 2 + [((NEAR, 2 * C), BF16), ((PTS, 6 * 128), BF16)],
        [SMEM, SMEM] + [VMEM] * 14,
        [((NEAR, C), F32), ((NEAR, C), BF16), ((NEAR, 2 * C), BF16)] + [((NWIN * WIN, 2 * C), BF16)] * 2
        + [(big, F32)] * 6 + [((ROWS, 128), F32)],
    )(lengths, place, near, gain, w_in, cotangent, qa, ka, va, da, kvb, qdb, xhat, normed_t,
      onehot, onehot_t)
    own, other = reduced(keep, send)
    d_near = d_near.reshape(3, 3, SAMP, 2 * C)
    upper = moved(d_near[:, 2], GY, 4, 1).astype(F32)
    lower = moved(d_near[:, 0], GY, 4, -1).astype(F32)
    partial_sum = d_near[:, 1].astype(F32) + upper + lower
    upper = moved(partial_sum[2].astype(BF16), GX, 64, 1).astype(F32)
    lower = moved(partial_sum[0].astype(BF16), GX, 64, -1).astype(F32)
    returned = (partial_sum[1] + upper + lower).astype(BF16)
    layer_out, feature_gradient = call(
        finish_kernel, [((PTS, C), BF16), ((PTS, C), F32)], [VMEM] * 7
    )(points, gain, w_in, w_back, cotangent, grads, returned)
    weights, gain_gradient = call(
        unpack_kernel, [((4, C, C), F32), ((1, C), F32)], [SMEM, VMEM, VMEM], [((ROWS, 128), F32)]
    )(place, own, other)
    return layer_out[None, None], feature_gradient[None, None], weights, gain_gradient.reshape(C)


def solution(mesh):
    inner = Mesh(mesh.devices.reshape(8, 4, 2, 2, 2), ("z", "y", "xl", "xh", "c"))
    return jax.shard_map(
        body,
        mesh=inner,
        in_specs=(P(GX, GY, None, None), P(), P(), P(), P(), P(), P(GX, GY, None),
                  P(GX, GY, None, None), P(GX, GY, None, None)),
        out_specs=(P(GX, GY, None, None), P(GX, GY, None, None), P(), P()),
        check_vma=False,
    )
```

```python
import jax
import jax.numpy as jnp
from jax import lax
from jax.experimental import pallas as pl
from jax.experimental.pallas import tpu as pltpu
from jax.sharding import Mesh, PartitionSpec as P

C = 192
H = 6
DEPTH = 32
PTS = 1024
WIN = 64
NWIN = 24
SAMP = 64
NEAR = 9 * SAMP
PAD = PTS + WIN
ROWS = 1280
CHUNK = ROWS // 32
GX = ("z", "y", "xl")
GY = ("xh", "c")
GROUP = ("c", "y", "xl", "xh")
SCALE = DEPTH ** (-0.5)
LOG2E = 1.4426950408889634
F32 = jnp.float32
BF16 = jnp.bfloat16
VMEM = pl.BlockSpec(memory_space=pltpu.VMEM)
SMEM = pl.BlockSpec(memory_space=pltpu.SMEM)
ANY = pl.BlockSpec(memory_space=pl.ANY)
UNROLL = 4


def nn(a, b):
    return lax.dot_general(a, b, (((1,), (0,)), ((), ())), preferred_element_type=F32)


def nt(a, b):
    return lax.dot_general(a, b, (((1,), (1,)), ((), ())), preferred_element_type=F32)


def tn(a, b):
    return lax.dot_general(a, b, (((0,), (0,)), ((), ())), preferred_element_type=F32)


def standardize(x, axis):
    mean = jnp.sum(x, axis=axis, keepdims=True) * (1.0 / C)
    centred = x - mean
    variance = jnp.sum(centred * centred, axis=axis, keepdims=True) * (1.0 / C)
    inverse = lax.rsqrt(variance + 1e-05)
    return centred * inverse, inverse


def sample_kernel(points, sample):
    row = lax.broadcasted_iota(jnp.int32, (SAMP, PTS), 0) * 16
    column = lax.broadcasted_iota(jnp.int32, (SAMP, PTS), 1)
    sample[...] = nt(jnp.where(row == column, 1.0, 0.0).astype(BF16), points[...]).astype(BF16)


def gain_column(gain):
    return jnp.broadcast_to(gain[...], (128, C)).T


def prepare_kernel(after, points, gain, wq, wk, wv, wo, cot, picks_row, picks_col,
                   qa, ka, va, da, kvb, qdb, normed_t, w_in, w_back, onehot, onehot_t):
    chunk = 128
    gain_t = gain_column(gain)
    empty = jnp.zeros((C, 64), BF16)
    back = wo[...].astype(F32).T.astype(BF16)
    w_in[:, 0:128] = wq[:, 0:128]
    w_in[:, 128:256] = wk[:, 0:128]
    w_in[:, 256:384] = wv[:, 0:128]
    w_in[:, 384:512] = jnp.concatenate([wk[:, 128:], wv[:, 128:]], axis=1)
    w_in[:, 512:640] = jnp.concatenate([wq[:, 128:], empty], axis=1)
    w_back[:, 0:128] = jnp.concatenate([empty, back[:, 128:]], axis=1)
    w_back[:, 128:256] = back[:, 0:128]

    def project(i, _):
        rows = pl.ds(pl.multiple_of(i * chunk, chunk), chunk)
        hat, _inv = standardize(points[:, rows].astype(F32), 0)
        normed = (hat * gain_t).astype(BF16)
        normed_t[:, rows] = normed
        wide = tn(normed, w_in[...])
        back = tn(cot[:, rows], w_back[...])
        for ref, x in ((qa, wide[:, :128]), (ka, wide[:, 128:256]), (va, wide[:, 256:384]),
                       (kvb, wide[:, 384:512]), (da, back[:, 128:]), (qdb, wide[:, 512:] + back[:, :128])):
            ref[rows, :] = x.astype(BF16).astype(F32)
        return 0

    lax.fori_loop(0, PTS // chunk, project, 0)
    zeros = jnp.zeros((WIN, 128), F32)
    for ref in (qa, ka, va, da, kvb, qdb):
        ref[PTS:, :] = zeros

    def rows_hot(i, _):
        rows = pl.ds(pl.multiple_of(i * WIN, WIN), WIN)
        ids = lax.broadcasted_iota(jnp.int32, (WIN, NEAR), 1)
        onehot[rows, :] = jnp.where(picks_col[rows, :] == ids, 1.0, 0.0).astype(BF16)
        return 0

    lax.fori_loop(0, NWIN, rows_hot, 0)

    def columns_hot(i, _):
        rows = pl.ds(pl.multiple_of(i * SAMP, SAMP), SAMP)
        ids = lax.broadcasted_iota(jnp.int32, (SAMP, NWIN * WIN), 0) + i * SAMP
        onehot_t[rows, :] = jnp.where(picks_row[...] == ids, 1.0, 0.0).astype(BF16)
        return 0

    lax.fori_loop(0, 9, columns_hot, 0)


def attend_kernel(lengths, low, middle, high, gain, w_in, qa, ka, va, da, kvb, qdb, onehot, onehot_t,
                  d_near, d_low, d_high, rest, grads, near_hat, near_normed,
                  near_kv, pick, d_pick, oa_s, dqa_s, dka_s, dva_s, dkvb_s, dqob_s):
    near_points = jnp.concatenate([low[...], middle[...], high[...]], axis=0)
    hat, _inv = standardize(near_points.astype(F32), 1)
    near_hat[...] = hat
    normed = (hat * gain[...]).astype(BF16)
    near_normed[...] = normed
    near_kv[...] = nn(normed, w_in[:, 128:512]).astype(BF16)

    def choose(i, _):
        rows = pl.ds(pl.multiple_of(i * 256, 256), 256)
        pick[rows, :] = nn(onehot[rows, :], near_kv[...]).astype(BF16)
        return 0

    lax.fori_loop(0, NWIN * WIN // 256, choose, 0)

    lane_head = lax.broadcasted_iota(jnp.int32, (1, 128), 1) // DEPTH
    lanes = [jnp.where(lane_head == h, 1.0, 0.0).astype(BF16) for h in range(4)]
    key_id = lax.broadcasted_iota(jnp.int32, (1, 128), 1)
    slot = lax.broadcasted_iota(jnp.int32, (WIN, 1), 0)
    half_scale = jnp.where(key_id < 64, SCALE, 1.0)

    def per_head(x):
        return jnp.concatenate([x * lane for lane in lanes], axis=0)

    def down(parts):
        return jnp.concatenate(parts, axis=0)

    def along(parts):
        return jnp.concatenate(parts, axis=1)

    def softmax(scores, bias):
        scores = scores + bias
        top = jnp.max(scores, axis=-1, keepdims=True)
        weights = jnp.exp2((scores - top) * (SCALE * LOG2E))
        return weights * (1.0 / jnp.sum(weights, axis=-1, keepdims=True))

    def score_gradient(probs, d_probs):
        d_probs = d_probs.astype(BF16).astype(F32)
        inner = jnp.sum(d_probs * probs, axis=-1, keepdims=True)
        return (probs * (d_probs - inner)).astype(BF16)

    def head(x, h):
        return x[:, 128 * h:128 * (h + 1)]

    def window(w, offset):
        count = lengths[w]
        rows = pl.ds(offset, WIN)
        own = pl.ds(pl.multiple_of(w * WIN, WIN), WIN)
        bias = jnp.where((key_id >= count) & (key_id < WIN), -1e30, 0.0)
        alive = slot < count
        keys = per_head(down([ka[rows, :].astype(BF16), pick[own, 0:128]]))
        values = per_head(down([va[rows, :].astype(BF16), pick[own, 128:256]]))
        both = per_head(down([kvb[rows, :].astype(BF16), pick[own, 256:384]]))
        q = qa[rows, :].astype(BF16)
        d = jnp.where(alive, da[rows, :], 0.0).astype(BF16)
        qd = jnp.where(alive, qdb[rows, :], 0.0).astype(BF16)
        scores = nt(q, keys)
        d_probs = nt(d, values)
        mixed = nt(qd, both)
        probs = [softmax(head(scores, h), bias) for h in range(4)]
        probs_b = [softmax(head(mixed, h), bias) for h in range(2)]
        probs16 = [p.astype(BF16) for p in probs]
        d_scores = [score_gradient(p, head(d_probs, h)) for h, p in enumerate(probs)]
        back = [score_gradient(p, head(mixed, 2 + h)) for h, p in enumerate(probs_b)]
        back = back + [p.astype(BF16) for p in probs_b]
        oa_s[rows, :] = nn(along(probs16), values)
        dqa_s[rows, :] = nn(along(d_scores), keys) * SCALE
        dqob_s[rows, :] = nn(along(back), both) * half_scale
        d_keys = tn(down(d_scores), per_head(q)) * SCALE
        d_values = tn(down(probs16), per_head(d))
        d_both = tn(down(back), per_head(qd)) * half_scale
        dka_s[rows, :] = d_keys[:WIN]
        dva_s[rows, :] = d_values[:WIN]
        dkvb_s[rows, :] = d_both[:WIN]
        d_pick[own, 0:128] = d_keys[WIN:].astype(BF16)
        d_pick[own, 128:256] = d_values[WIN:].astype(BF16)
        d_pick[own, 256:384] = d_both[WIN:].astype(BF16)
        return offset + count

    lax.fori_loop(0, NWIN, window, jnp.int32(0), unroll=UNROLL)

    near = nn(onehot_t[...], d_pick[...])
    near16 = near.astype(BF16)
    d_near[...] = near16
    for i in range(3):
        d_low[i] = near16[192 * i:192 * i + 64]
        d_high[i] = near16[192 * i + 128:192 * i + 192]
    rest[...] = (near - near16.astype(F32)).astype(BF16)
    for i, ref in enumerate((dqa_s, dka_s, dva_s, dkvb_s, dqob_s, oa_s)):
        grads[:, 128 * i:128 * (i + 1)] = ref[:PTS, :].astype(BF16)


def weights_kernel(points, cot, w_in, normed_t, grads, d_near, rest, near_hat, near_normed, packed):
    wide = nn(normed_t[...], grads[:, 0:640])
    near_wide = tn(near_normed[...], d_near[...]) + tn(near_normed[...], rest[...])
    out = nn(cot[...], grads[:, 512:768])
    packed[0:192, :] = wide[:, 0:128]
    packed[192:384, :] = wide[:, 128:256] + near_wide[:, 0:128]
    packed[384:576, :] = wide[:, 256:384] + near_wide[:, 128:256]
    packed[576:768, :] = out[:, 128:256]
    packed[768:960, :] = wide[:, 384:512] + near_wide[:, 256:384]
    lane = lax.broadcasted_iota(jnp.int32, (C, 128), 1)
    packed[960:1152, :] = jnp.where(lane < 64, wide[:, 512:640], out[:, 0:128])

    def gain_part(i, total):
        rows = pl.ds(pl.multiple_of(i * 128, 128), 128)
        hat, _inv = standardize(points[:, rows].astype(F32), 0)
        return total + nt(w_in[...], grads[rows, 0:640]) * hat

    total = lax.fori_loop(0, PTS // 128, gain_part, jnp.zeros((C, 128), F32))
    w_kv = w_in[:, 128:512]
    d = nt(d_near[...], w_kv) + nt(rest[...], w_kv)
    near_total = jnp.sum((d * near_hat[...]).reshape(NEAR // 8, 8, C), axis=0)
    gain_sum = jnp.sum(total.T, axis=0, keepdims=True) + jnp.sum(near_total, axis=0, keepdims=True)
    packed[1152:, :] = jnp.zeros((ROWS - 1152, 128), F32)
    packed[1152:1153, :] = gain_sum[:, :128]
    packed[1153:1154, 0:64] = gain_sum[:, 128:]


def sides_kernel(d_near, upper, lower, up, down, middle):
    def side(i):
        own = d_near[192 * i + 64:192 * i + 128, :].astype(F32)
        return own + upper[i].astype(F32) + lower[i].astype(F32)

    up[...] = side(2).astype(BF16)
    down[...] = side(0).astype(BF16)
    middle[...] = side(1)


def fold_kernel(upper, lower, parts, out):
    total = parts[0]
    for i in range(1, parts.shape[0]):
        total = total + parts[i]
    for i in range(out.shape[0]):
        out[i] = total


def finish_kernel(points, gain, w_in, w_back, cot, grads, middle, upper, lower,
                  layer_out, feature_gradient, token, returned):
    token[...] = jnp.zeros(token.shape, F32)
    chunk = 128
    returned[...] = (middle[...] + upper[...].astype(F32) + lower[...].astype(F32)).astype(BF16)
    gain_t = gain_column(gain)

    def part(i, _):
        rows = pl.ds(pl.multiple_of(i * chunk, chunk), chunk)
        x = points[:, rows].astype(F32)
        hat, inverse = standardize(x, 0)
        row = lax.broadcasted_iota(jnp.int32, (chunk, SAMP), 0) + i * chunk
        column = lax.broadcasted_iota(jnp.int32, (chunk, SAMP), 1)
        spread = jnp.where(row == column * 16, 1.0, 0.0).astype(BF16)
        total = (grads[rows, 128:512].astype(F32) + nn(spread, returned[...])).astype(BF16)
        d = nt(w_in[:, 0:128], grads[rows, 0:128]) + nt(w_in[:, 128:512], total)
        d = d + nt(w_in[:, 512:640], grads[rows, 512:640])
        d = d * gain_t
        mean = jnp.sum(d, axis=0, keepdims=True) * (1.0 / C)
        along = jnp.sum(d * hat, axis=0, keepdims=True) * (1.0 / C)
        feature_gradient[:, rows] = inverse * (d - mean - hat * along) + cot[:, rows].astype(F32)
        layer_out[:, rows] = (x + nt(w_back[...], grads[rows, 512:768])).astype(BF16)
        return 0

    lax.fori_loop(0, PTS // chunk, part, 0)


def unpack_kernel(after, gathered, weights, gain_gradient, packed):
    packed[...] = gathered[...] * (PTS * 256) ** (-0.5)
    for i, (tail, side) in enumerate(((960, 0), (768, 0), (768, 64))):
        weights[i, :, 0:128] = packed[192 * i:192 * (i + 1), :]
        weights[i, :, 128:C] = packed[tail:tail + 192, side:side + 64]
    weights[3, 0:128, :] = packed[576:768, :].T
    weights[3, 128:C, :] = packed[960:1152, :].T[64:128, :]
    gain_gradient[:, 0:128] = packed[1152:1153, :]
    gain_gradient[:, 128:C] = packed[1153:1154, 0:64]


def call(kernel, outs, specs, scratch=(), limit=24, micros=1.0):
    return pl.pallas_call(
        kernel,
        out_shape=[jax.ShapeDtypeStruct(s, t) for s, t in outs],
        in_specs=specs,
        out_specs=[VMEM] * len(outs),
        scratch_shapes=[pltpu.VMEM(s, t) for s, t in scratch],
        cost_estimate=pl.CostEstimate(flops=int(micros * 1e9), bytes_accessed=int(micros * 3e6), transcendentals=0),
        compiler_params=pltpu.CompilerParams(vmem_limit_bytes=limit * 1024 * 1024),
    )


def moved(block, axes, count, distance):
    route = [(i, (i + distance) % count) for i in range(count)]
    return lax.ppermute(block, axes, route)


def extended(rows, axes, count):
    return jnp.concatenate([moved(rows, axes, count, 1), rows, moved(rows, axes, count, -1)], axis=0)


def exchanged(x, axes):
    return lax.all_to_all(x, axes, 0, 0, tiled=True)


def local_prepare(after, points, gain, w_query, w_key, w_value, w_out, cotangent, picks):
    big = ((PAD, 128), F32)
    outs = [big] * 6 + [((C, PTS), BF16), ((C, 640), BF16), ((C, 256), BF16)]
    outs = outs + [((NWIN * WIN, NEAR), BF16), ((NEAR, NWIN * WIN), BF16)]
    return call(prepare_kernel, outs, [ANY] + [VMEM] * 9, limit=24, micros=5.0)(
        after, points, gain.reshape(1, C), w_query, w_key, w_value, w_out, cotangent,
        picks.reshape(1, NWIN * WIN), picks.reshape(NWIN * WIN, 1))


def local_attend(lengths, near, gain, w_in, projections, hots):
    big = ((PAD, 128), F32)
    near_out = ((NEAR, 2 * C), BF16)
    return call(
        attend_kernel,
        [near_out] + [((3, SAMP, 2 * C), BF16)] * 2 + [near_out, ((PTS, 6 * 128), BF16), ((NEAR, C), F32), ((NEAR, C), BF16)],
        [SMEM] + [VMEM] * 13,
        [near_out] + [((NWIN * WIN, 2 * C), BF16)] * 2 + [big] * 6,
        limit=26, micros=18.0,
    )(lengths, *near, gain.reshape(1, C), w_in, *projections, *hots)


def local_weights(points, cotangent, w_in, normed_t, grads, d_near, rest, near_hat, near_normed):
    return call(
        weights_kernel, [((ROWS, 128), F32)], [VMEM] * 9, limit=14, micros=3.0
    )(points, cotangent, w_in, normed_t, grads, d_near, rest, near_hat, near_normed)[0]


def local_finish(points, gain, w_in, w_back, cotangent, grads, middle, upper, lower):
    outs = [((C, PTS), BF16), ((C, PTS), F32), ((8, 128), F32)]
    return call(finish_kernel, outs, [VMEM] * 9, [((SAMP, 2 * C), BF16)], limit=12, micros=4.0)(
        points, gain.reshape(1, C), w_in, w_back, cotangent, grads, middle, upper, lower)


def local_sides(d_near, upper, lower):
    outs = [((SAMP, 2 * C), BF16)] * 2 + [((SAMP, 2 * C), F32)]
    return call(sides_kernel, outs, [VMEM] * 3, limit=6)(d_near, upper, lower)


def local_fold(upper, lower, parts, copies):
    outs = [((copies,) + parts.shape[1:], F32)]
    return call(fold_kernel, outs, [ANY, ANY, VMEM], limit=6)(upper, lower, parts)[0]


def local_unpack(after, gathered):
    return call(
        unpack_kernel, [((4, C, C), F32), ((1, C), F32)], [ANY, VMEM], [((ROWS, 128), F32)],
        limit=8, micros=1.0,
    )(after, gathered)


def body(points, gain, w_query, w_key, w_value, w_out, lengths, picks, cotangent):
    points = points[0, 0].T
    cotangent = cotangent[0, 0].T
    lengths = lengths.reshape(NWIN)
    sample = call(sample_kernel, [((SAMP, C), BF16)], [VMEM], limit=6)(points)[0]
    across = extended(sample, GY, 4)
    near = (moved(across, GX, 64, 1), across, moved(across, GX, 64, -1))
    *projections, normed_t, w_in, w_back, onehot, onehot_t = local_prepare(
        across, points, gain, w_query, w_key, w_value, w_out, cotangent, picks)
    hots = (onehot, onehot_t)
    d_near, d_low, d_high, rest, grads, near_hat, near_normed = local_attend(
        lengths, near, gain, w_in, projections, hots)
    upper = moved(d_high, GY, 4, 1)
    lower = moved(d_low, GY, 4, -1)
    packed = local_weights(points, cotangent, w_in, normed_t, grads, d_near, rest, near_hat, near_normed)
    mixed = exchanged(packed.reshape(32, CHUNK, 128), GROUP)
    mixed = exchanged(local_fold(upper, lower, mixed, 8), "z")
    up, down, middle = local_sides(d_near, upper, lower)
    upper = moved(up, GX, 64, 1)
    lower = moved(down, GX, 64, -1)
    gathered = exchanged(local_fold(upper, lower, mixed, 32), GROUP).reshape(ROWS, 128)
    layer_out, feature_gradient, token = local_finish(
        points, gain, w_in, w_back, cotangent, grads, middle, upper, lower)
    weights, gain_gradient = local_unpack(token, gathered)
    return layer_out.T[None, None], feature_gradient.T[None, None], weights, gain_gradient.reshape(C)


def solution(mesh):
    inner = Mesh(mesh.devices.reshape(8, 4, 2, 2, 2), ("z", "y", "xl", "xh", "c"))
    return jax.shard_map(
        body,
        mesh=inner,
        in_specs=(P(GX, GY, None, None), P(), P(), P(), P(), P(), P(GX, GY, None),
                  P(GX, GY, None, None), P(GX, GY, None, None)),
        out_specs=(P(GX, GY, None, None), P(GX, GY, None, None), P(), P()),
        check_vma=False,
    )
```

```python
import jax
import jax.numpy as jnp
from jax import lax
from jax.experimental import pallas as pl
from jax.experimental.pallas import tpu as pltpu
from jax.sharding import Mesh, PartitionSpec as P

C = 192
H = 6
DEPTH = 32
PTS = 1024
WIN = 64
NWIN = 24
SAMP = 64
NEAR = 9 * SAMP
PAD = PTS + WIN
ROWS = 1280
HALF = ROWS // 2
GX = ("z", "y", "xl")
GY = ("xh", "c")
XY = ("y", "xl", "xh")
SCALE = DEPTH ** (-0.5)
LOG2E = 1.4426950408889634
F32 = jnp.float32
BF16 = jnp.bfloat16
VMEM = pl.BlockSpec(memory_space=pltpu.VMEM)
SMEM = pl.BlockSpec(memory_space=pltpu.SMEM)
ANY = pl.BlockSpec(memory_space=pl.ANY)
TOGETHER = 4


def nn(a, b):
    return lax.dot_general(a, b, (((1,), (0,)), ((), ())), preferred_element_type=F32)


def nt(a, b):
    return lax.dot_general(a, b, (((1,), (1,)), ((), ())), preferred_element_type=F32)


def tn(a, b):
    return lax.dot_general(a, b, (((0,), (0,)), ((), ())), preferred_element_type=F32)


def standardize(x, axis):
    mean = jnp.sum(x, axis=axis, keepdims=True) * (1.0 / C)
    centred = x - mean
    variance = jnp.sum(centred * centred, axis=axis, keepdims=True) * (1.0 / C)
    inverse = lax.rsqrt(variance + 1e-05)
    return centred * inverse, inverse


def sample_kernel(points, sample):
    row = lax.broadcasted_iota(jnp.int32, (SAMP, PTS), 0) * 16
    column = lax.broadcasted_iota(jnp.int32, (SAMP, PTS), 1)
    sample[...] = nt(jnp.where(row == column, 1.0, 0.0).astype(BF16), points[...]).astype(BF16)


def gain_column(gain):
    return jnp.broadcast_to(gain[...], (128, C)).T


def order_kernel(place, own, first, second, across):
    odd = place[1]
    across[SAMP:2 * SAMP, :] = own[...]
    across[pl.ds(pl.multiple_of(2 * SAMP * (1 - odd), SAMP), SAMP), :] = first[...]
    across[pl.ds(pl.multiple_of(2 * SAMP * odd, SAMP), SAMP), :] = second[...]


def prepare_kernel(after, points, gain, wq, wk, wv, wo, cot, picks_row, picks_col,
                   qa, ka, va, da, kvb, qdb, normed_t, w_in, w_back, onehot, onehot_t):
    chunk = 128
    gain_t = gain_column(gain)
    empty = jnp.zeros((C, 64), BF16)
    back = wo[...].astype(F32).T.astype(BF16)
    w_in[:, 0:128] = wq[:, 0:128]
    w_in[:, 128:256] = wk[:, 0:128]
    w_in[:, 256:384] = wv[:, 0:128]
    w_in[:, 384:512] = jnp.concatenate([wk[:, 128:], wv[:, 128:]], axis=1)
    w_in[:, 512:640] = jnp.concatenate([wq[:, 128:], empty], axis=1)
    w_back[:, 0:128] = jnp.concatenate([empty, back[:, 128:]], axis=1)
    w_back[:, 128:256] = back[:, 0:128]

    def project(i, _):
        rows = pl.ds(pl.multiple_of(i * chunk, chunk), chunk)
        hat, _inv = standardize(points[:, rows].astype(F32), 0)
        normed = (hat * gain_t).astype(BF16)
        normed_t[:, rows] = normed
        wide = tn(normed, w_in[...])
        back = tn(cot[:, rows], w_back[...])
        for ref, x in ((qa, wide[:, :128]), (ka, wide[:, 128:256]), (va, wide[:, 256:384]),
                       (kvb, wide[:, 384:512]), (da, back[:, 128:]), (qdb, wide[:, 512:] + back[:, :128])):
            ref[rows, :] = x.astype(BF16).astype(F32)
        return 0

    lax.fori_loop(0, PTS // chunk, project, 0)
    zeros = jnp.zeros((WIN, 128), F32)
    for ref in (qa, ka, va, da, kvb, qdb):
        ref[PTS:, :] = zeros

    def rows_hot(i, _):
        rows = pl.ds(pl.multiple_of(i * WIN, WIN), WIN)
        ids = lax.broadcasted_iota(jnp.int32, (WIN, NEAR), 1)
        onehot[rows, :] = jnp.where(picks_col[rows, :] == ids, 1.0, 0.0).astype(BF16)
        return 0

    lax.fori_loop(0, NWIN, rows_hot, 0)

    def columns_hot(i, _):
        rows = pl.ds(pl.multiple_of(i * SAMP, SAMP), SAMP)
        ids = lax.broadcasted_iota(jnp.int32, (SAMP, NWIN * WIN), 0) + i * SAMP
        onehot_t[rows, :] = jnp.where(picks_row[...] == ids, 1.0, 0.0).astype(BF16)
        return 0

    lax.fori_loop(0, 9, columns_hot, 0)


def attend_kernel(lengths, place, own_near, first, second, gain, w_in, qa, ka, va, da, kvb, qdb, onehot, onehot_t,
                  d_near, d_first, d_second, rest, grads, near_hat, near_normed,
                  near_points, near_kv, pick, d_pick, oa_s, dqa_s, dka_s, dva_s, dkvb_s, dqob_s):
    odd = place[0]
    strip = 3 * SAMP
    near_points[strip:2 * strip, :] = own_near[...]
    near_points[pl.ds(pl.multiple_of(2 * strip * (1 - odd), SAMP), strip), :] = first[...]
    near_points[pl.ds(pl.multiple_of(2 * strip * odd, SAMP), strip), :] = second[...]
    hat, _inv = standardize(near_points[...].astype(F32), 1)
    near_hat[...] = hat
    normed = (hat * gain[...]).astype(BF16)
    near_normed[...] = normed
    near_kv[...] = nn(normed, w_in[:, 128:512]).astype(BF16)

    def choose(i, _):
        rows = pl.ds(pl.multiple_of(i * 256, 256), 256)
        pick[rows, :] = nn(onehot[rows, :], near_kv[...]).astype(BF16)
        return 0

    lax.fori_loop(0, NWIN * WIN // 256, choose, 0)

    lane_head = lax.broadcasted_iota(jnp.int32, (1, 128), 1) // DEPTH
    lanes = [jnp.where(lane_head == h, 1.0, 0.0).astype(BF16) for h in range(4)]
    key_id = lax.broadcasted_iota(jnp.int32, (1, 128), 1)
    slot = lax.broadcasted_iota(jnp.int32, (WIN, 1), 0)
    half_scale = jnp.where(key_id < 64, SCALE, 1.0)

    def per_head(x):
        return jnp.concatenate([x * lane for lane in lanes], axis=0)

    def down(parts):
        return jnp.concatenate(parts, axis=0)

    def softmax(scores, bias):
        scores = scores + bias
        top = jnp.max(scores, axis=-1, keepdims=True)
        weights = jnp.exp2((scores - top) * (SCALE * LOG2E))
        return weights * (1.0 / jnp.sum(weights, axis=-1, keepdims=True))

    def score_gradient(probs, d_probs):
        d_probs = d_probs.astype(BF16).astype(F32)
        inner = jnp.sum(d_probs * probs, axis=-1, keepdims=True)
        return (probs * (d_probs - inner)).astype(BF16)

    def cut(x):
        return [x[WIN * h:WIN * (h + 1)] for h in range(4)]

    def merge(x):
        parts = [part * lane for part, lane in zip(cut(x), lanes32)]
        return (parts[0] + parts[1]) + (parts[2] + parts[3])

    lanes32 = [lane.astype(F32) for lane in lanes]

    def load(w, offset):
        count = lengths[w]
        rows = pl.ds(offset, WIN)
        own = pl.ds(pl.multiple_of(w * WIN, WIN), WIN)
        bias = jnp.where((key_id >= count) & (key_id < WIN), -1e30, 0.0)
        alive = slot < count
        keys = down([ka[rows, :].astype(BF16), pick[own, 0:128]])
        values = down([va[rows, :].astype(BF16), pick[own, 128:256]])
        both = down([kvb[rows, :].astype(BF16), pick[own, 256:384]])
        qe = per_head(qa[rows, :].astype(BF16))
        de = per_head(jnp.where(alive, da[rows, :], 0.0).astype(BF16))
        qde = per_head(jnp.where(alive, qdb[rows, :], 0.0).astype(BF16))
        return rows, own, bias, keys, values, both, qe, de, qde

    def scored(item):
        _, _, _, keys, values, both, qe, de, qde = item
        return nt(qe, keys), nt(de, values), nt(qde, both)

    def weighed(item, found):
        bias = item[2]
        scores, d_probs, mixed = [cut(x) for x in found]
        probs = [softmax(x, bias) for x in scores]
        probs_b = [softmax(x, bias) for x in mixed[:2]]
        d_scores = [score_gradient(p, x) for p, x in zip(probs, d_probs)]
        back = [score_gradient(p, x) for p, x in zip(probs_b, mixed[2:])]
        back = back + [p.astype(BF16) for p in probs_b]
        return down([p.astype(BF16) for p in probs]), down(d_scores), down(back)

    def stored(item, found):
        rows, own, _, keys, values, both, qe, de, qde = item
        probs, d_scores, back = found
        oa_s[rows, :] = merge(nn(probs, values))
        dqa_s[rows, :] = merge(nn(d_scores, keys)) * SCALE
        dqob_s[rows, :] = merge(nn(back, both)) * half_scale
        d_keys = tn(d_scores, qe) * SCALE
        d_values = tn(probs, de)
        d_both = tn(back, qde) * half_scale
        dka_s[rows, :] = d_keys[:WIN]
        dva_s[rows, :] = d_values[:WIN]
        dkvb_s[rows, :] = d_both[:WIN]
        d_pick[own, 0:128] = d_keys[WIN:].astype(BF16)
        d_pick[own, 128:256] = d_values[WIN:].astype(BF16)
        d_pick[own, 256:384] = d_both[WIN:].astype(BF16)

    def windows(group, offset):
        items = []
        for j in range(TOGETHER):
            items.append(load(group * TOGETHER + j, offset))
            offset = offset + lengths[group * TOGETHER + j]
        found = [scored(item) for item in items]
        found = [weighed(item, x) for item, x in zip(items, found)]
        for item, x in zip(items, found):
            stored(item, x)
        return offset

    lax.fori_loop(0, NWIN // TOGETHER, windows, jnp.int32(0))

    near = nn(onehot_t[...], d_pick[...])
    near16 = near.astype(BF16)
    d_near[...] = near16
    side = place[1]
    for i in range(3):
        d_first[i] = d_near[pl.ds(pl.multiple_of(192 * i + 128 * (1 - side), SAMP), SAMP), :]
        d_second[i] = d_near[pl.ds(pl.multiple_of(192 * i + 128 * side, SAMP), SAMP), :]
    rest[...] = (near - near16.astype(F32)).astype(BF16)
    for i, ref in enumerate((dqa_s, dka_s, dva_s, dkvb_s, dqob_s, oa_s)):
        grads[:, 128 * i:128 * (i + 1)] = ref[:PTS, :].astype(BF16)


def weights_kernel(points, cot, w_in, normed_t, grads, wide, out, gain_sum):
    wide[...] = nn(normed_t[...], grads[:, 0:640])
    out[...] = nn(cot[...], grads[:, 512:768])

    def gain_part(i, total):
        rows = pl.ds(pl.multiple_of(i * 128, 128), 128)
        hat, _inv = standardize(points[:, rows].astype(F32), 0)
        return total + nt(w_in[...], grads[rows, 0:640]) * hat

    total = lax.fori_loop(0, PTS // 128, gain_part, jnp.zeros((C, 128), F32))
    gain_sum[...] = jnp.sum(total.T, axis=0, keepdims=True)


def near_kernel(place, w_in, wide, out, gain_sum, d_near, rest, near_hat, near_normed, got, got_too,
                keep, send, first, second, middle, packed, sides):
    near_wide = tn(near_normed[...], d_near[...]) + tn(near_normed[...], rest[...])
    packed[0:192, :] = wide[:, 0:128]
    packed[192:384, :] = wide[:, 128:256] + near_wide[:, 0:128]
    packed[384:576, :] = wide[:, 256:384] + near_wide[:, 128:256]
    packed[576:768, :] = out[:, 128:256]
    packed[768:960, :] = wide[:, 384:512] + near_wide[:, 256:384]
    lane = lax.broadcasted_iota(jnp.int32, (C, 128), 1)
    packed[960:1152, :] = jnp.where(lane < 64, wide[:, 512:640], out[:, 0:128])
    w_kv = w_in[:, 128:512]
    d = nt(d_near[...], w_kv) + nt(rest[...], w_kv)
    near_total = jnp.sum((d * near_hat[...]).reshape(NEAR // 8, 8, C), axis=0)
    gains = gain_sum[...] + jnp.sum(near_total, axis=0, keepdims=True)
    packed[1152:, :] = jnp.zeros((ROWS - 1152, 128), F32)
    packed[1152:1153, :] = gains[:, :128]
    packed[1153:1154, 0:64] = gains[:, 128:]
    for i in range(3):
        own = d_near[192 * i + 64:192 * i + 128, :].astype(F32)
        sides[SAMP * i:SAMP * (i + 1), :] = own + got[i].astype(F32) + got_too[i].astype(F32)
    odd = place[0]
    first[...] = sides[pl.ds(pl.multiple_of(2 * SAMP * (1 - odd), SAMP), SAMP), :].astype(BF16)
    second[...] = sides[pl.ds(pl.multiple_of(2 * SAMP * odd, SAMP), SAMP), :].astype(BF16)
    middle[...] = sides[SAMP:2 * SAMP, :]
    mine = place[1]
    keep[...] = packed[pl.ds(pl.multiple_of(mine * HALF, HALF), HALF), :]
    send[...] = packed[pl.ds(pl.multiple_of((1 - mine) * HALF, HALF), HALF), :]


def fold_kernel(after, parts, out):
    total = parts[0]
    for i in range(1, parts.shape[0]):
        total = total + parts[i]
    for i in range(out.shape[0]):
        out[i] = total


def finish_kernel(points, gain, w_in, w_back, cot, grads, middle, upper, lower,
                  layer_out, feature_gradient, token, returned):
    token[...] = jnp.zeros(token.shape, F32)
    chunk = 128
    returned[...] = (middle[...] + upper[...].astype(F32) + lower[...].astype(F32)).astype(BF16)
    gain_t = gain_column(gain)

    def part(i, _):
        rows = pl.ds(pl.multiple_of(i * chunk, chunk), chunk)
        x = points[:, rows].astype(F32)
        hat, inverse = standardize(x, 0)
        row = lax.broadcasted_iota(jnp.int32, (chunk, SAMP), 0) + i * chunk
        column = lax.broadcasted_iota(jnp.int32, (chunk, SAMP), 1)
        spread = jnp.where(row == column * 16, 1.0, 0.0).astype(BF16)
        total = (grads[rows, 128:512].astype(F32) + nn(spread, returned[...])).astype(BF16)
        d = nt(w_in[:, 0:128], grads[rows, 0:128]) + nt(w_in[:, 128:512], total)
        d = d + nt(w_in[:, 512:640], grads[rows, 512:640])
        d = d * gain_t
        mean = jnp.sum(d, axis=0, keepdims=True) * (1.0 / C)
        along = jnp.sum(d * hat, axis=0, keepdims=True) * (1.0 / C)
        feature_gradient[:, rows] = inverse * (d - mean - hat * along) + cot[:, rows].astype(F32)
        layer_out[:, rows] = (x + nt(w_back[...], grads[rows, 512:768])).astype(BF16)
        return 0

    lax.fori_loop(0, PTS // chunk, part, 0)


def unpack_kernel(place, own, other, weights, gain_gradient, packed):
    mine = place[1]
    factor = (PTS * 256) ** (-0.5)
    packed[pl.ds(pl.multiple_of(mine * HALF, HALF), HALF), :] = own[...] * factor
    packed[pl.ds(pl.multiple_of((1 - mine) * HALF, HALF), HALF), :] = other[...] * factor
    for i, (tail, side) in enumerate(((960, 0), (768, 0), (768, 64))):
        weights[i, :, 0:128] = packed[192 * i:192 * (i + 1), :]
        weights[i, :, 128:C] = packed[tail:tail + 192, side:side + 64]
    weights[3, 0:128, :] = packed[576:768, :].T
    weights[3, 128:C, :] = packed[960:1152, :].T[64:128, :]
    gain_gradient[:, 0:128] = packed[1152:1153, :]
    gain_gradient[:, 128:C] = packed[1153:1154, 0:64]


def call(kernel, outs, specs, scratch=(), limit=24, micros=1.0):
    return pl.pallas_call(
        kernel,
        out_shape=[jax.ShapeDtypeStruct(s, t) for s, t in outs],
        in_specs=specs,
        out_specs=[VMEM] * len(outs),
        scratch_shapes=[pltpu.VMEM(s, t) for s, t in scratch],
        cost_estimate=pl.CostEstimate(flops=int(micros * 1e9), bytes_accessed=int(micros * 3e6), transcendentals=0),
        compiler_params=pltpu.CompilerParams(vmem_limit_bytes=limit * 1024 * 1024),
    )


def neighbours(first, second, axes, count):
    pairs = [(i, i ^ 1) for i in range(count)]
    across = [(i, min(max(((i + 1) ^ 1) - 1, 0), count - 1)) for i in range(count)]
    return lax.ppermute(first, axes, pairs), lax.ppermute(second, axes, across)


def swapped(x):
    return lax.ppermute(x, "c", [(0, 1), (1, 0)])


def exchanged(x, axes):
    return lax.all_to_all(x, axes, 0, 0, tiled=True)


def local_prepare(after, points, gain, w_query, w_key, w_value, w_out, cotangent, picks):
    big = ((PAD, 128), F32)
    outs = [big] * 6 + [((C, PTS), BF16), ((C, 640), BF16), ((C, 256), BF16)]
    outs = outs + [((NWIN * WIN, NEAR), BF16), ((NEAR, NWIN * WIN), BF16)]
    return call(prepare_kernel, outs, [ANY] + [VMEM] * 9, limit=24, micros=5.0)(
        after, points, gain.reshape(1, C), w_query, w_key, w_value, w_out, cotangent,
        picks.reshape(1, NWIN * WIN), picks.reshape(NWIN * WIN, 1))


def local_order(place, own, first, second):
    return call(order_kernel, [((3 * SAMP, C), BF16)], [SMEM] + [VMEM] * 3, limit=6)(
        place, own, first, second)[0]


def local_attend(lengths, place, near, gain, w_in, projections, hots):
    big = ((PAD, 128), F32)
    near_out = ((NEAR, 2 * C), BF16)
    side = ((3, SAMP, 2 * C), BF16)
    return call(
        attend_kernel,
        [near_out, side, side, near_out, ((PTS, 6 * 128), BF16), ((NEAR, C), F32), ((NEAR, C), BF16)],
        [SMEM] * 2 + [VMEM] * 13,
        [((NEAR, C), BF16), near_out] + [((NWIN * WIN, 2 * C), BF16)] * 2 + [big] * 6,
        limit=26, micros=14.0,
    )(lengths, place, *near, gain.reshape(1, C), w_in, *projections, *hots)


def local_weights(points, cotangent, w_in, normed_t, grads):
    outs = [((C, 640), F32), ((C, 256), F32), ((1, C), F32)]
    return call(weights_kernel, outs, [VMEM] * 5, limit=12, micros=3.0)(
        points, cotangent, w_in, normed_t, grads)


def local_near(place, w_in, sums, d_near, rest, near_hat, near_normed, got):
    side = ((SAMP, 2 * C), BF16)
    outs = [((HALF, 128), F32)] * 2 + [side, side, ((SAMP, 2 * C), F32)]
    scratch = [((ROWS, 128), F32), ((3 * SAMP, 2 * C), F32)]
    return call(near_kernel, outs, [SMEM] + [VMEM] * 10, scratch, limit=12)(
        place, w_in, *sums, d_near, rest, near_hat, near_normed, *got)


def local_finish(points, gain, w_in, w_back, cotangent, grads, middle, upper, lower):
    outs = [((C, PTS), BF16), ((C, PTS), F32), ((8, 128), F32)]
    return call(finish_kernel, outs, [VMEM] * 9, [((SAMP, 2 * C), BF16)], limit=12, micros=4.0)(
        points, gain.reshape(1, C), w_in, w_back, cotangent, grads, middle, upper, lower)


def local_fold(after, parts, copies):
    outs = [((copies,) + parts.shape[1:], F32)]
    return call(fold_kernel, outs, [ANY, VMEM], limit=6)(after, parts)[0]


def local_unpack(place, own, other):
    return call(
        unpack_kernel, [((4, C, C), F32), ((1, C), F32)], [SMEM, VMEM, VMEM], [((ROWS, 128), F32)],
        limit=8, micros=1.0,
    )(place, own, other)


def body(points, gain, w_query, w_key, w_value, w_out, lengths, picks, cotangent):
    points = points[0, 0].T
    cotangent = cotangent[0, 0].T
    lengths = lengths.reshape(NWIN)
    sample = call(sample_kernel, [((SAMP, C), BF16)], [VMEM], limit=6)(points)[0]
    place = jnp.stack([lax.axis_index("xl"), lax.axis_index("c")]).astype(jnp.int32)
    across = local_order(place, sample, *neighbours(sample, sample, GY, 4))
    near = (across,) + neighbours(across, across, GX, 64)
    *projections, normed_t, w_in, w_back, onehot, onehot_t = local_prepare(
        across, points, gain, w_query, w_key, w_value, w_out, cotangent, picks)
    hots = (onehot, onehot_t)
    d_near, d_first, d_second, rest, grads, near_hat, near_normed = local_attend(
        lengths, place, near, gain, w_in, projections, hots)
    got = neighbours(d_first, d_second, GY, 4)
    sums = local_weights(points, cotangent, w_in, normed_t, grads)
    keep, send, first, second, middle = local_near(
        place, w_in, sums, d_near, rest, near_hat, near_normed, got)
    got = neighbours(first, second, GX, 64)
    layer_out, feature_gradient, token = local_finish(
        points, gain, w_in, w_back, cotangent, grads, middle, *got)
    mixed = exchanged((keep + swapped(send)).reshape(16, HALF // 16, 128), XY)
    mixed = exchanged(local_fold(got[0], mixed, 8), "z")
    own = exchanged(local_fold(token, mixed, 16), XY).reshape(HALF, 128)
    weights, gain_gradient = local_unpack(place, own, swapped(own))
    return layer_out.T[None, None], feature_gradient.T[None, None], weights, gain_gradient.reshape(C)


def solution(mesh):
    inner = Mesh(mesh.devices.reshape(8, 4, 2, 2, 2), ("z", "y", "xl", "xh", "c"))
    return jax.shard_map(
        body,
        mesh=inner,
        in_specs=(P(GX, GY, None, None), P(), P(), P(), P(), P(), P(GX, GY, None),
                  P(GX, GY, None, None), P(GX, GY, None, None)),
        out_specs=(P(GX, GY, None, None), P(GX, GY, None, None), P(), P()),
        check_vma=False,
    )
```

```python
import jax
import jax.numpy as jnp
from jax import lax
from jax.experimental import pallas as pl
from jax.experimental.pallas import tpu as pltpu
from jax.sharding import Mesh, PartitionSpec as P

C = 192
H = 6
DEPTH = 32
PTS = 1024
WIN = 64
NWIN = 24
SAMP = 64
NEAR = 9 * SAMP
PAD = PTS + WIN
ROWS = 1280
HALF = ROWS // 2
GX = ("z", "y", "xl")
GY = ("xh", "c")
XY = ("y", "xl", "xh")
SCALE = DEPTH ** (-0.5)
LOG2E = 1.4426950408889634
F32 = jnp.float32
BF16 = jnp.bfloat16
VMEM = pl.BlockSpec(memory_space=pltpu.VMEM)
SMEM = pl.BlockSpec(memory_space=pltpu.SMEM)
ANY = pl.BlockSpec(memory_space=pl.ANY)
TOGETHER = 6


def nn(a, b):
    return lax.dot_general(a, b, (((1,), (0,)), ((), ())), preferred_element_type=F32)


def nt(a, b):
    return lax.dot_general(a, b, (((1,), (1,)), ((), ())), preferred_element_type=F32)


def tn(a, b):
    return lax.dot_general(a, b, (((0,), (0,)), ((), ())), preferred_element_type=F32)


def standardize(x, axis):
    mean = jnp.sum(x, axis=axis, keepdims=True) * (1.0 / C)
    centred = x - mean
    variance = jnp.sum(centred * centred, axis=axis, keepdims=True) * (1.0 / C)
    inverse = lax.rsqrt(variance + 1e-05)
    return centred * inverse, inverse


def sample_kernel(points, sample):
    row = lax.broadcasted_iota(jnp.int32, (SAMP, PTS), 0) * 16
    column = lax.broadcasted_iota(jnp.int32, (SAMP, PTS), 1)
    sample[...] = nt(jnp.where(row == column, 1.0, 0.0).astype(BF16), points[...]).astype(BF16)


def gain_column(gain):
    return jnp.broadcast_to(gain[...], (128, C)).T


def order_kernel(place, own, first, second, across):
    odd = place[1]
    across[SAMP:2 * SAMP, :] = own[...]
    across[pl.ds(pl.multiple_of(2 * SAMP * (1 - odd), SAMP), SAMP), :] = first[...]
    across[pl.ds(pl.multiple_of(2 * SAMP * odd, SAMP), SAMP), :] = second[...]


def prepare_kernel(after, points, gain, wq, wk, wv, wo, cot, picks_row, picks_col,
                   qa, ka, va, da, kvb, qdb, normed_t, w_in, w_back, onehot, onehot_t):
    chunk = 128
    gain_t = gain_column(gain)
    empty = jnp.zeros((C, 64), BF16)
    back = wo[...].astype(F32).T.astype(BF16)
    w_in[:, 0:128] = wq[:, 0:128]
    w_in[:, 128:256] = wk[:, 0:128]
    w_in[:, 256:384] = wv[:, 0:128]
    w_in[:, 384:512] = jnp.concatenate([wk[:, 128:], wv[:, 128:]], axis=1)
    w_in[:, 512:640] = jnp.concatenate([wq[:, 128:], empty], axis=1)
    w_back[:, 0:128] = jnp.concatenate([empty, back[:, 128:]], axis=1)
    w_back[:, 128:256] = back[:, 0:128]

    def project(i, _):
        rows = pl.ds(pl.multiple_of(i * chunk, chunk), chunk)
        hat, _inv = standardize(points[:, rows].astype(F32), 0)
        normed = (hat * gain_t).astype(BF16)
        normed_t[:, rows] = normed
        wide = tn(normed, w_in[...])
        back = tn(cot[:, rows], w_back[...])
        for ref, x in ((qa, wide[:, :128]), (ka, wide[:, 128:256]), (va, wide[:, 256:384]),
                       (kvb, wide[:, 384:512]), (da, back[:, 128:]), (qdb, wide[:, 512:] + back[:, :128])):
            ref[rows, :] = x.astype(BF16).astype(F32)
        return 0

    lax.fori_loop(0, PTS // chunk, project, 0, unroll=8)
    zeros = jnp.zeros((WIN, 128), F32)
    for ref in (qa, ka, va, da, kvb, qdb):
        ref[PTS:, :] = zeros

    def rows_hot(i, _):
        rows = pl.ds(pl.multiple_of(i * WIN, WIN), WIN)
        ids = lax.broadcasted_iota(jnp.int32, (WIN, NEAR), 1)
        onehot[rows, :] = jnp.where(picks_col[rows, :] == ids, 1.0, 0.0).astype(BF16)
        return 0

    lax.fori_loop(0, NWIN, rows_hot, 0, unroll=12)

    def columns_hot(i, _):
        rows = pl.ds(pl.multiple_of(i * SAMP, SAMP), SAMP)
        ids = lax.broadcasted_iota(jnp.int32, (SAMP, NWIN * WIN), 0) + i * SAMP
        onehot_t[rows, :] = jnp.where(picks_row[...] == ids, 1.0, 0.0).astype(BF16)
        return 0

    lax.fori_loop(0, 9, columns_hot, 0, unroll=9)


def attend_kernel(lengths, place, own_near, first, second, gain, w_in, qa, ka, va, da, kvb, qdb, onehot, onehot_t,
                  d_near, d_first, d_second, rest, grads, near_hat, near_normed,
                  near_points, near_kv, pick, d_pick, oa_s, dqa_s, dka_s, dva_s, dkvb_s, dqob_s):
    odd = place[0]
    strip = 3 * SAMP
    near_points[strip:2 * strip, :] = own_near[...]
    near_points[pl.ds(pl.multiple_of(2 * strip * (1 - odd), SAMP), strip), :] = first[...]
    near_points[pl.ds(pl.multiple_of(2 * strip * odd, SAMP), strip), :] = second[...]
    hat, _inv = standardize(near_points[...].astype(F32), 1)
    near_hat[...] = hat
    normed = (hat * gain[...]).astype(BF16)
    near_normed[...] = normed
    near_kv[...] = nn(normed, w_in[:, 128:512]).astype(BF16)

    def choose(group):
        size = TOGETHER * WIN
        rows = pl.ds(pl.multiple_of(group * size, size), size)
        pick[rows, :] = nn(onehot[rows, :], near_kv[...]).astype(BF16)

    choose(0)

    lane_head = lax.broadcasted_iota(jnp.int32, (1, 128), 1) // DEPTH
    lanes = [jnp.where(lane_head == h, 1.0, 0.0).astype(BF16) for h in range(4)]
    key_id = lax.broadcasted_iota(jnp.int32, (1, 128), 1)
    slot = lax.broadcasted_iota(jnp.int32, (WIN, 1), 0)
    half_scale = jnp.where(key_id < 64, SCALE, 1.0)

    def per_head(x):
        return jnp.concatenate([x * lane for lane in lanes], axis=0)

    def down(parts):
        return jnp.concatenate(parts, axis=0)

    ones = jnp.ones((256, 128), BF16)

    def row_sum(x):
        high = x.astype(BF16)
        low = (x - high.astype(F32)).astype(BF16)
        return nn(jnp.concatenate([high, low], axis=1), ones)

    def softmax(scores, bias):
        scores = scores + bias
        top = jnp.max(scores, axis=-1, keepdims=True)
        weights = jnp.exp2((scores - top) * (SCALE * LOG2E))
        return weights * (1.0 / jnp.sum(weights, axis=-1, keepdims=True))

    def score_gradient(probs, d_probs):
        d_probs = d_probs.astype(BF16).astype(F32)
        inner = row_sum(d_probs * probs)
        return (probs * (d_probs - inner)).astype(BF16)

    def cut(x):
        return [x[WIN * h:WIN * (h + 1)] for h in range(4)]

    def merge(x):
        parts = [part * lane for part, lane in zip(cut(x), lanes32)]
        return (parts[0] + parts[1]) + (parts[2] + parts[3])

    lanes32 = [lane.astype(F32) for lane in lanes]

    def load(w, offset):
        count = lengths[w]
        rows = pl.ds(offset, WIN)
        own = pl.ds(pl.multiple_of(w * WIN, WIN), WIN)
        bias = jnp.where((key_id >= count) & (key_id < WIN), -1e30, 0.0)
        alive = slot < count
        keys = down([ka[rows, :].astype(BF16), pick[own, 0:128]])
        values = down([va[rows, :].astype(BF16), pick[own, 128:256]])
        both = down([kvb[rows, :].astype(BF16), pick[own, 256:384]])
        qe = per_head(qa[rows, :].astype(BF16))
        de = per_head(jnp.where(alive, da[rows, :], 0.0).astype(BF16))
        qde = per_head(jnp.where(alive, qdb[rows, :], 0.0).astype(BF16))
        return rows, own, bias, keys, values, both, qe, de, qde

    def scored(item):
        _, _, _, keys, values, both, qe, de, qde = item
        return nt(qe, keys), nt(de, values), nt(qde, both)

    def weighed(item, found):
        bias = item[2]
        scores, d_probs, mixed = [cut(x) for x in found]
        probs = [softmax(x, bias) for x in scores]
        probs_b = [softmax(x, bias) for x in mixed[:2]]
        d_scores = [score_gradient(p, x) for p, x in zip(probs, d_probs)]
        back = [score_gradient(p, x) for p, x in zip(probs_b, mixed[2:])]
        back = back + [p.astype(BF16) for p in probs_b]
        return down([p.astype(BF16) for p in probs]), down(d_scores), down(back)

    def stored(item, found):
        rows, own, _, keys, values, both, qe, de, qde = item
        probs, d_scores, back = found
        oa_s[rows, :] = merge(nn(probs, values))
        dqa_s[rows, :] = merge(nn(d_scores, keys)) * SCALE
        dqob_s[rows, :] = merge(nn(back, both)) * half_scale
        d_keys = tn(d_scores, qe) * SCALE
        d_values = tn(probs, de)
        d_both = tn(back, qde) * half_scale
        dka_s[rows, :] = d_keys[:WIN]
        dva_s[rows, :] = d_values[:WIN]
        dkvb_s[rows, :] = d_both[:WIN]
        d_pick[own, 0:128] = d_keys[WIN:].astype(BF16)
        d_pick[own, 128:256] = d_values[WIN:].astype(BF16)
        d_pick[own, 256:384] = d_both[WIN:].astype(BF16)

    def windows(group, offset):
        items = []
        for j in range(TOGETHER):
            items.append(load(group * TOGETHER + j, offset))
            offset = offset + lengths[group * TOGETHER + j]
        found = [scored(item) for item in items]
        choose(lax.rem(group + 1, NWIN // TOGETHER))
        found = [weighed(item, x) for item, x in zip(items, found)]
        for item, x in zip(items, found):
            stored(item, x)
        return offset

    lax.fori_loop(0, NWIN // TOGETHER, windows, jnp.int32(0))

    near = nn(onehot_t[...], d_pick[...])
    near16 = near.astype(BF16)
    d_near[...] = near16
    side = place[1]
    for i in range(3):
        d_first[i] = d_near[pl.ds(pl.multiple_of(192 * i + 128 * (1 - side), SAMP), SAMP), :]
        d_second[i] = d_near[pl.ds(pl.multiple_of(192 * i + 128 * side, SAMP), SAMP), :]
    rest[...] = (near - near16.astype(F32)).astype(BF16)
    for i, ref in enumerate((dqa_s, dka_s, dva_s, dkvb_s, dqob_s, oa_s)):
        grads[:, 128 * i:128 * (i + 1)] = ref[:PTS, :].astype(BF16)


def weights_kernel(points, cot, w_in, normed_t, grads, d_near, rest, near_hat, near_normed, place,
                   keep, send, packed):
    wide = nn(normed_t[...], grads[:, 0:640])
    out = nn(cot[...], grads[:, 512:768])
    near_wide = tn(near_normed[...], jnp.concatenate([d_near[...], rest[...]], axis=1))
    near_wide = near_wide[:, 0:384] + near_wide[:, 384:768]
    packed[0:192, :] = wide[:, 0:128]
    packed[192:384, :] = wide[:, 128:256] + near_wide[:, 0:128]
    packed[384:576, :] = wide[:, 256:384] + near_wide[:, 128:256]
    packed[576:768, :] = out[:, 128:256]
    packed[768:960, :] = wide[:, 384:512] + near_wide[:, 256:384]
    lane = lax.broadcasted_iota(jnp.int32, (C, 128), 1)
    packed[960:1152, :] = jnp.where(lane < 64, wide[:, 512:640], out[:, 0:128])

    def gain_part(i, total):
        rows = pl.ds(pl.multiple_of(i * 128, 128), 128)
        hat, _inv = standardize(points[:, rows].astype(F32), 0)
        return total + nt(w_in[...], grads[rows, 0:640]) * hat

    total = lax.fori_loop(0, PTS // 128, gain_part, jnp.zeros((C, 128), F32), unroll=8)
    w_kv = w_in[:, 128:512]
    d = nt(d_near[...], w_kv) + nt(rest[...], w_kv)
    near_total = jnp.sum((d * near_hat[...]).reshape(NEAR // 8, 8, C), axis=0)
    gains = jnp.sum(total.T, axis=0, keepdims=True) + jnp.sum(near_total, axis=0, keepdims=True)
    packed[1152:, :] = jnp.zeros((ROWS - 1152, 128), F32)
    packed[1152:1153, :] = gains[:, :128]
    packed[1153:1154, 0:64] = gains[:, 128:]
    mine = place[1]
    keep[...] = packed[pl.ds(pl.multiple_of(mine * HALF, HALF), HALF), :]
    send[...] = packed[pl.ds(pl.multiple_of((1 - mine) * HALF, HALF), HALF), :]


def sides_kernel(place, send, d_near, got, got_too, same, first, second, middle, sides):
    for i in range(3):
        own = d_near[192 * i + 64:192 * i + 128, :].astype(F32)
        sides[SAMP * i:SAMP * (i + 1), :] = own + got[i].astype(F32) + got_too[i].astype(F32)
    odd = place[0]
    first[...] = sides[pl.ds(pl.multiple_of(2 * SAMP * (1 - odd), SAMP), SAMP), :].astype(BF16)
    second[...] = sides[pl.ds(pl.multiple_of(2 * SAMP * odd, SAMP), SAMP), :].astype(BF16)
    middle[...] = sides[SAMP:2 * SAMP, :]


def fold_kernel(after, parts, out):
    total = parts[0]
    for i in range(1, parts.shape[0]):
        total = total + parts[i]
    for i in range(out.shape[0]):
        out[i] = total


def finish_kernel(points, gain, w_in, w_back, cot, grads, middle, upper, lower,
                  layer_out, feature_gradient, token, returned):
    token[...] = jnp.zeros(token.shape, F32)
    chunk = 128
    returned[...] = (middle[...] + upper[...].astype(F32) + lower[...].astype(F32)).astype(BF16)
    gain_t = gain_column(gain)

    def part(i, _):
        rows = pl.ds(pl.multiple_of(i * chunk, chunk), chunk)
        x = points[:, rows].astype(F32)
        hat, inverse = standardize(x, 0)
        row = lax.broadcasted_iota(jnp.int32, (chunk, SAMP), 0) + i * chunk
        column = lax.broadcasted_iota(jnp.int32, (chunk, SAMP), 1)
        spread = jnp.where(row == column * 16, 1.0, 0.0).astype(BF16)
        total = (grads[rows, 128:512].astype(F32) + nn(spread, returned[...])).astype(BF16)
        d = nt(w_in[:, 0:128], grads[rows, 0:128]) + nt(w_in[:, 128:512], total)
        d = d + nt(w_in[:, 512:640], grads[rows, 512:640])
        d = d * gain_t
        mean = jnp.sum(d, axis=0, keepdims=True) * (1.0 / C)
        along = jnp.sum(d * hat, axis=0, keepdims=True) * (1.0 / C)
        feature_gradient[:, rows] = inverse * (d - mean - hat * along) + cot[:, rows].astype(F32)
        layer_out[:, rows] = (x + nt(w_back[...], grads[rows, 512:768])).astype(BF16)
        return 0

    lax.fori_loop(0, PTS // chunk, part, 0, unroll=8)


def unpack_kernel(place, own, other, weights, gain_gradient, packed):
    mine = place[1]
    factor = (PTS * 256) ** (-0.5)
    packed[pl.ds(pl.multiple_of(mine * HALF, HALF), HALF), :] = own[...] * factor
    packed[pl.ds(pl.multiple_of((1 - mine) * HALF, HALF), HALF), :] = other[...] * factor
    for i, (tail, side) in enumerate(((960, 0), (768, 0), (768, 64))):
        weights[i, :, 0:128] = packed[192 * i:192 * (i + 1), :]
        weights[i, :, 128:C] = packed[tail:tail + 192, side:side + 64]
    weights[3, 0:128, :] = packed[576:768, :].T
    weights[3, 128:C, :] = packed[960:1152, :].T[64:128, :]
    gain_gradient[:, 0:128] = packed[1152:1153, :]
    gain_gradient[:, 128:C] = packed[1153:1154, 0:64]


def call(kernel, outs, specs, scratch=(), limit=24, micros=1.0, aliases=None):
    return pl.pallas_call(
        kernel,
        out_shape=[jax.ShapeDtypeStruct(s, t) for s, t in outs],
        in_specs=specs,
        out_specs=[ANY if i in (aliases or {}).values() else VMEM for i in range(len(outs))],
        input_output_aliases=aliases or {},
        scratch_shapes=[pltpu.VMEM(s, t) for s, t in scratch],
        cost_estimate=pl.CostEstimate(flops=int(micros * 1e9), bytes_accessed=int(micros * 3e6), transcendentals=0),
        compiler_params=pltpu.CompilerParams(vmem_limit_bytes=limit * 1024 * 1024),
    )


def neighbours(first, second, axes, count):
    pairs = [(i, i ^ 1) for i in range(count)]
    across = [(i, min(max(((i + 1) ^ 1) - 1, 0), count - 1)) for i in range(count)]
    return lax.ppermute(first, axes, pairs), lax.ppermute(second, axes, across)


def swapped(x):
    return lax.ppermute(x, "c", [(0, 1), (1, 0)])


def exchanged(x, axes):
    return lax.all_to_all(x, axes, 0, 0, tiled=True)


def local_prepare(after, points, gain, w_query, w_key, w_value, w_out, cotangent, picks):
    big = ((PAD, 128), F32)
    outs = [big] * 6 + [((C, PTS), BF16), ((C, 640), BF16), ((C, 256), BF16)]
    outs = outs + [((NWIN * WIN, NEAR), BF16), ((NEAR, NWIN * WIN), BF16)]
    return call(prepare_kernel, outs, [ANY] + [VMEM] * 9, limit=24, micros=5.0)(
        after, points, gain.reshape(1, C), w_query, w_key, w_value, w_out, cotangent,
        picks.reshape(1, NWIN * WIN), picks.reshape(NWIN * WIN, 1))


def local_order(place, own, first, second):
    return call(order_kernel, [((3 * SAMP, C), BF16)], [SMEM] + [VMEM] * 3, limit=6)(
        place, own, first, second)[0]


def local_attend(lengths, place, near, gain, w_in, projections, hots):
    big = ((PAD, 128), F32)
    near_out = ((NEAR, 2 * C), BF16)
    side = ((3, SAMP, 2 * C), BF16)
    return call(
        attend_kernel,
        [near_out, side, side, near_out, ((PTS, 6 * 128), BF16), ((NEAR, C), F32), ((NEAR, C), BF16)],
        [SMEM] * 2 + [VMEM] * 13,
        [((NEAR, C), BF16), near_out] + [((NWIN * WIN, 2 * C), BF16)] * 2 + [big] * 6,
        limit=26, micros=14.0,
    )(lengths, place, *near, gain.reshape(1, C), w_in, *projections, *hots)


def local_weights(points, cotangent, w_in, normed_t, grads, d_near, rest, near_hat, near_normed, place):
    return call(weights_kernel, [((HALF, 128), F32)] * 2, [VMEM] * 9 + [SMEM], [((ROWS, 128), F32)],
                limit=14, micros=3.0)(
        points, cotangent, w_in, normed_t, grads, d_near, rest, near_hat, near_normed, place)


def local_sides(place, send, d_near, got):
    side = ((SAMP, 2 * C), BF16)
    outs = [((HALF, 128), F32), side, side, ((SAMP, 2 * C), F32)]
    return call(sides_kernel, outs, [SMEM, ANY] + [VMEM] * 3, [((3 * SAMP, 2 * C), F32)], limit=6,
                aliases={1: 0})(place, send, d_near, *got)


def local_finish(points, gain, w_in, w_back, cotangent, grads, middle, upper, lower):
    outs = [((C, PTS), BF16), ((C, PTS), F32), ((8, 128), F32)]
    return call(finish_kernel, outs, [VMEM] * 9, [((SAMP, 2 * C), BF16)], limit=12, micros=4.0)(
        points, gain.reshape(1, C), w_in, w_back, cotangent, grads, middle, upper, lower)


def local_fold(after, parts, copies):
    outs = [((copies,) + parts.shape[1:], F32)]
    return call(fold_kernel, outs, [ANY, VMEM], limit=6)(after, parts)[0]


def local_unpack(place, own, other):
    return call(
        unpack_kernel, [((4, C, C), F32), ((1, C), F32)], [SMEM, VMEM, VMEM], [((ROWS, 128), F32)],
        limit=8, micros=1.0,
    )(place, own, other)


def body(points, gain, w_query, w_key, w_value, w_out, lengths, picks, cotangent):
    points = points[0, 0].T
    cotangent = cotangent[0, 0].T
    lengths = lengths.reshape(NWIN)
    sample = call(sample_kernel, [((SAMP, C), BF16)], [VMEM], limit=6)(points)[0]
    place = jnp.stack([lax.axis_index("xl"), lax.axis_index("c")]).astype(jnp.int32)
    across = local_order(place, sample, *neighbours(sample, sample, GY, 4))
    near = (across,) + neighbours(across, across, GX, 64)
    *projections, normed_t, w_in, w_back, onehot, onehot_t = local_prepare(
        across, points, gain, w_query, w_key, w_value, w_out, cotangent, picks)
    hots = (onehot, onehot_t)
    d_near, d_first, d_second, rest, grads, near_hat, near_normed = local_attend(
        lengths, place, near, gain, w_in, projections, hots)
    got = neighbours(d_first, d_second, GY, 4)
    keep, send = local_weights(
        points, cotangent, w_in, normed_t, grads, d_near, rest, near_hat, near_normed, place)
    send, first, second, middle = local_sides(place, send, d_near, got)
    got = neighbours(first, second, GX, 64)
    layer_out, feature_gradient, token = local_finish(
        points, gain, w_in, w_back, cotangent, grads, middle, *got)
    mixed = exchanged((keep + swapped(send)).reshape(16, HALF // 16, 128), XY)
    mixed = exchanged(local_fold(got[0], mixed, 8), "z")
    own = exchanged(local_fold(token, mixed, 16), XY).reshape(HALF, 128)
    weights, gain_gradient = local_unpack(place, own, swapped(own))
    return layer_out.T[None, None], feature_gradient.T[None, None], weights, gain_gradient.reshape(C)


def solution(mesh):
    inner = Mesh(mesh.devices.reshape(8, 4, 2, 2, 2), ("z", "y", "xl", "xh", "c"))
    return jax.shard_map(
        body,
        mesh=inner,
        in_specs=(P(GX, GY, None, None), P(), P(), P(), P(), P(), P(GX, GY, None),
                  P(GX, GY, None, None), P(GX, GY, None, None)),
        out_specs=(P(GX, GY, None, None), P(GX, GY, None, None), P(), P()),
        check_vma=False,
    )
```

```python
import jax
import jax.numpy as jnp
from jax import lax
from jax.experimental import pallas as pl
from jax.experimental.pallas import tpu as pltpu
from jax.sharding import Mesh, PartitionSpec as P

C = 192
H = 6
DEPTH = 32
PTS = 1024
WIN = 64
NWIN = 24
SAMP = 64
NEAR = 9 * SAMP
PAD = PTS + WIN
ROWS = 1280
HALF = ROWS // 2
GX = ("z", "y", "xl")
GY = ("xh", "c")
XY = ("y", "xl", "xh")
SCALE = DEPTH ** (-0.5)
LOG2E = 1.4426950408889634
F32 = jnp.float32
BF16 = jnp.bfloat16
VMEM = pl.BlockSpec(memory_space=pltpu.VMEM)
SMEM = pl.BlockSpec(memory_space=pltpu.SMEM)
ANY = pl.BlockSpec(memory_space=pl.ANY)
TOGETHER = 6


def nn(a, b):
    return lax.dot_general(a, b, (((1,), (0,)), ((), ())), preferred_element_type=F32)


def nt(a, b):
    return lax.dot_general(a, b, (((1,), (1,)), ((), ())), preferred_element_type=F32)


def tn(a, b):
    return lax.dot_general(a, b, (((0,), (0,)), ((), ())), preferred_element_type=F32)


def standardize(x, axis):
    mean = jnp.sum(x, axis=axis, keepdims=True) * (1.0 / C)
    centred = x - mean
    variance = jnp.sum(centred * centred, axis=axis, keepdims=True) * (1.0 / C)
    inverse = lax.rsqrt(variance + 1e-05)
    return centred * inverse, inverse


def sample_kernel(points, sample):
    row = lax.broadcasted_iota(jnp.int32, (SAMP, PTS), 0) * 16
    column = lax.broadcasted_iota(jnp.int32, (SAMP, PTS), 1)
    sample[...] = nt(jnp.where(row == column, 1.0, 0.0).astype(BF16), points[...]).astype(BF16)


def gain_column(gain):
    return jnp.broadcast_to(gain[...], (128, C)).T


def order_kernel(place, own, first, second, across):
    odd = place[1]
    across[SAMP:2 * SAMP, :] = own[...]
    across[pl.ds(pl.multiple_of(2 * SAMP * (1 - odd), SAMP), SAMP), :] = first[...]
    across[pl.ds(pl.multiple_of(2 * SAMP * odd, SAMP), SAMP), :] = second[...]


def prepare_kernel(after, points, gain, wq, wk, wv, wo, cot, picks_row, picks_col,
                   qa, ka, va, da, kvb, qdb, normed_t, w_in, w_back, onehot, onehot_t):
    chunk = 128
    gain_t = gain_column(gain)
    empty = jnp.zeros((C, 64), BF16)
    back = wo[...].astype(F32).T.astype(BF16)
    w_in[:, 0:128] = wq[:, 0:128]
    w_in[:, 128:256] = wk[:, 0:128]
    w_in[:, 256:384] = wv[:, 0:128]
    w_in[:, 384:512] = jnp.concatenate([wk[:, 128:], wv[:, 128:]], axis=1)
    w_in[:, 512:640] = jnp.concatenate([wq[:, 128:], empty], axis=1)
    w_back[:, 0:128] = jnp.concatenate([empty, back[:, 128:]], axis=1)
    w_back[:, 128:256] = back[:, 0:128]

    def project(i, _):
        rows = pl.ds(pl.multiple_of(i * chunk, chunk), chunk)
        hat, _inv = standardize(points[:, rows].astype(F32), 0)
        normed = (hat * gain_t).astype(BF16)
        normed_t[:, rows] = normed
        wide = tn(normed, w_in[...])
        back = tn(cot[:, rows], w_back[...])
        for ref, x in ((qa, wide[:, :128]), (ka, wide[:, 128:256]), (va, wide[:, 256:384]),
                       (kvb, wide[:, 384:512]), (da, back[:, 128:]), (qdb, wide[:, 512:] + back[:, :128])):
            ref[rows, :] = x.astype(BF16).astype(F32)
        return 0

    lax.fori_loop(0, PTS // chunk, project, 0, unroll=8)
    zeros = jnp.zeros((WIN, 128), F32)
    for ref in (qa, ka, va, da, kvb, qdb):
        ref[PTS:, :] = zeros

    def rows_hot(i, _):
        rows = pl.ds(pl.multiple_of(i * WIN, WIN), WIN)
        ids = lax.broadcasted_iota(jnp.int32, (WIN, NEAR), 1)
        onehot[rows, :] = jnp.where(picks_col[rows, :] == ids, 1.0, 0.0).astype(BF16)
        return 0

    lax.fori_loop(0, NWIN, rows_hot, 0, unroll=12)

    def columns_hot(i, _):
        rows = pl.ds(pl.multiple_of(i * SAMP, SAMP), SAMP)
        ids = lax.broadcasted_iota(jnp.int32, (SAMP, NWIN * WIN), 0) + i * SAMP
        onehot_t[rows, :] = jnp.where(picks_row[...] == ids, 1.0, 0.0).astype(BF16)
        return 0

    lax.fori_loop(0, 9, columns_hot, 0, unroll=9)


def attend_kernel(lengths, place, own_near, first, second, gain, w_in, qa, ka, va, da, kvb, qdb, onehot, onehot_t,
                  d_near, d_first, d_second, rest, grads, near_hat, near_normed,
                  near_points, near_kv, pick, d_pick, oa_s, dqa_s, dka_s, dva_s, dkvb_s, dqob_s):
    odd = place[0]
    strip = 3 * SAMP
    near_points[strip:2 * strip, :] = own_near[...]
    near_points[pl.ds(pl.multiple_of(2 * strip * (1 - odd), SAMP), strip), :] = first[...]
    near_points[pl.ds(pl.multiple_of(2 * strip * odd, SAMP), strip), :] = second[...]
    hat, _inv = standardize(near_points[...].astype(F32), 1)
    near_hat[...] = hat
    normed = (hat * gain[...]).astype(BF16)
    near_normed[...] = normed
    near_kv[...] = nn(normed, w_in[:, 128:512]).astype(BF16)

    def choose(group):
        size = TOGETHER * WIN
        rows = pl.ds(pl.multiple_of(group * size, size), size)
        pick[rows, :] = nn(onehot[rows, :], near_kv[...]).astype(BF16)

    choose(0)

    lane_head = lax.broadcasted_iota(jnp.int32, (1, 128), 1) // DEPTH
    lanes = [jnp.where(lane_head == h, 1.0, 0.0).astype(BF16) for h in range(4)]
    key_id = lax.broadcasted_iota(jnp.int32, (1, 128), 1)
    slot = lax.broadcasted_iota(jnp.int32, (WIN, 1), 0)
    half_scale = jnp.where(key_id < 64, SCALE, 1.0)

    def per_head(x):
        return jnp.concatenate([x * lane for lane in lanes], axis=0)

    def down(parts):
        return jnp.concatenate(parts, axis=0)

    ones = jnp.ones((256, 128), BF16)

    def row_sum(x):
        high = x.astype(BF16)
        low = (x - high.astype(F32)).astype(BF16)
        return nn(jnp.concatenate([high, low], axis=1), ones)

    def softmax(scores, bias):
        scores = scores + bias
        top = jnp.max(scores, axis=-1, keepdims=True)
        weights = jnp.exp2((scores - top) * (SCALE * LOG2E))
        return weights * (1.0 / jnp.sum(weights, axis=-1, keepdims=True))

    def score_gradient(probs, d_probs):
        d_probs = d_probs.astype(BF16).astype(F32)
        inner = row_sum(d_probs * probs)
        return (probs * (d_probs - inner)).astype(BF16)

    def cut(x):
        return [x[WIN * h:WIN * (h + 1)] for h in range(4)]

    def merge(x):
        parts = [part * lane for part, lane in zip(cut(x), lanes32)]
        return (parts[0] + parts[1]) + (parts[2] + parts[3])

    lanes32 = [lane.astype(F32) for lane in lanes]

    def load(w, offset):
        count = lengths[w]
        rows = pl.ds(offset, WIN)
        own = pl.ds(pl.multiple_of(w * WIN, WIN), WIN)
        bias = jnp.where((key_id >= count) & (key_id < WIN), -1e30, 0.0)
        alive = slot < count
        keys = down([ka[rows, :].astype(BF16), pick[own, 0:128]])
        values = down([va[rows, :].astype(BF16), pick[own, 128:256]])
        both = down([kvb[rows, :].astype(BF16), pick[own, 256:384]])
        qe = per_head(qa[rows, :].astype(BF16))
        de = per_head(jnp.where(alive, da[rows, :], 0.0).astype(BF16))
        qde = per_head(jnp.where(alive, qdb[rows, :], 0.0).astype(BF16))
        return rows, own, bias, keys, values, both, qe, de, qde

    def scored(item):
        _, _, _, keys, values, both, qe, de, qde = item
        return nt(qe, keys), nt(de, values), nt(qde, both)

    def weighed(item, found):
        bias = item[2]
        scores, d_probs, mixed = [cut(x) for x in found]
        probs = [softmax(x, bias) for x in scores]
        probs_b = [softmax(x, bias) for x in mixed[:2]]
        d_scores = [score_gradient(p, x) for p, x in zip(probs, d_probs)]
        back = [score_gradient(p, x) for p, x in zip(probs_b, mixed[2:])]
        back = back + [p.astype(BF16) for p in probs_b]
        return down([p.astype(BF16) for p in probs]), down(d_scores), down(back)

    def stored(item, found):
        rows, own, _, keys, values, both, qe, de, qde = item
        probs, d_scores, back = found
        oa_s[rows, :] = merge(nn(probs, values))
        dqa_s[rows, :] = merge(nn(d_scores, keys)) * SCALE
        dqob_s[rows, :] = merge(nn(back, both)) * half_scale
        d_keys = tn(d_scores, qe) * SCALE
        d_values = tn(probs, de)
        d_both = tn(back, qde) * half_scale
        dka_s[rows, :] = d_keys[:WIN]
        dva_s[rows, :] = d_values[:WIN]
        dkvb_s[rows, :] = d_both[:WIN]
        d_pick[own, 0:128] = d_keys[WIN:].astype(BF16)
        d_pick[own, 128:256] = d_values[WIN:].astype(BF16)
        d_pick[own, 256:384] = d_both[WIN:].astype(BF16)

    def windows(group, offset):
        items = []
        for j in range(TOGETHER):
            items.append(load(group * TOGETHER + j, offset))
            offset = offset + lengths[group * TOGETHER + j]
        found = [scored(item) for item in items]
        choose(lax.rem(group + 1, NWIN // TOGETHER))
        found = [weighed(item, x) for item, x in zip(items, found)]
        for item, x in zip(items, found):
            stored(item, x)
        return offset

    lax.fori_loop(0, NWIN // TOGETHER, windows, jnp.int32(0))

    near = nn(onehot_t[...], d_pick[...])
    near16 = near.astype(BF16)
    d_near[...] = near16
    side = place[1]
    for i in range(3):
        d_first[i] = d_near[pl.ds(pl.multiple_of(192 * i + 128 * (1 - side), SAMP), SAMP), :]
        d_second[i] = d_near[pl.ds(pl.multiple_of(192 * i + 128 * side, SAMP), SAMP), :]
    rest[...] = (near - near16.astype(F32)).astype(BF16)
    for i, ref in enumerate((dqa_s, dka_s, dva_s, dkvb_s, dqob_s, oa_s)):
        grads[:, 128 * i:128 * (i + 1)] = ref[:PTS, :].astype(BF16)


def weights_kernel(points, cot, w_in, normed_t, grads, d_near, rest, near_hat, near_normed, place,
                   keep, send, packed):
    wide = nn(normed_t[...], grads[:, 0:640])
    out = nn(cot[...], grads[:, 512:768])
    near_wide = tn(near_normed[...], jnp.concatenate([d_near[...], rest[...]], axis=1))
    near_wide = near_wide[:, 0:384] + near_wide[:, 384:768]
    packed[0:192, :] = wide[:, 0:128]
    packed[192:384, :] = wide[:, 128:256] + near_wide[:, 0:128]
    packed[384:576, :] = wide[:, 256:384] + near_wide[:, 128:256]
    packed[576:768, :] = out[:, 128:256]
    packed[768:960, :] = wide[:, 384:512] + near_wide[:, 256:384]
    lane = lax.broadcasted_iota(jnp.int32, (C, 128), 1)
    packed[960:1152, :] = jnp.where(lane < 64, wide[:, 512:640], out[:, 0:128])

    def gain_part(i, total):
        rows = pl.ds(pl.multiple_of(i * 128, 128), 128)
        hat, _inv = standardize(points[:, rows].astype(F32), 0)
        return total + nt(w_in[...], grads[rows, 0:640]) * hat

    total = lax.fori_loop(0, PTS // 128, gain_part, jnp.zeros((C, 128), F32), unroll=8)
    w_kv = w_in[:, 128:512]
    d = nt(d_near[...], w_kv) + nt(rest[...], w_kv)
    near_total = jnp.sum((d * near_hat[...]).reshape(NEAR // 8, 8, C), axis=0)
    gains = jnp.sum(total.T, axis=0, keepdims=True) + jnp.sum(near_total, axis=0, keepdims=True)
    packed[1152:, :] = jnp.zeros((ROWS - 1152, 128), F32)
    packed[1152:1153, :] = gains[:, :128]
    packed[1153:1154, 0:64] = gains[:, 128:]
    mine = place[1]
    keep[...] = packed[pl.ds(pl.multiple_of(mine * HALF, HALF), HALF), :]
    send[...] = packed[pl.ds(pl.multiple_of((1 - mine) * HALF, HALF), HALF), :]


def sides_kernel(place, d_near, got, got_too, first, second, middle, sides):
    for i in range(3):
        own = d_near[192 * i + 64:192 * i + 128, :].astype(F32)
        sides[SAMP * i:SAMP * (i + 1), :] = own + got[i].astype(F32) + got_too[i].astype(F32)
    odd = place[0]
    first[...] = sides[pl.ds(pl.multiple_of(2 * SAMP * (1 - odd), SAMP), SAMP), :].astype(BF16)
    second[...] = sides[pl.ds(pl.multiple_of(2 * SAMP * odd, SAMP), SAMP), :].astype(BF16)
    middle[...] = sides[SAMP:2 * SAMP, :]


def fold_kernel(after, parts, out):
    total = parts[0]
    for i in range(1, parts.shape[0]):
        total = total + parts[i]
    for i in range(out.shape[0]):
        out[i] = total


def finish_kernel(points, gain, w_in, w_back, cot, grads, middle, upper, lower,
                  layer_out, feature_gradient, token, returned):
    token[...] = jnp.zeros(token.shape, F32)
    chunk = 128
    returned[...] = (middle[...] + upper[...].astype(F32) + lower[...].astype(F32)).astype(BF16)
    gain_t = gain_column(gain)

    def part(i, _):
        rows = pl.ds(pl.multiple_of(i * chunk, chunk), chunk)
        x = points[:, rows].astype(F32)
        hat, inverse = standardize(x, 0)
        row = lax.broadcasted_iota(jnp.int32, (chunk, SAMP), 0) + i * chunk
        column = lax.broadcasted_iota(jnp.int32, (chunk, SAMP), 1)
        spread = jnp.where(row == column * 16, 1.0, 0.0).astype(BF16)
        total = (grads[rows, 128:512].astype(F32) + nn(spread, returned[...])).astype(BF16)
        d = nt(w_in[:, 0:128], grads[rows, 0:128]) + nt(w_in[:, 128:512], total)
        d = d + nt(w_in[:, 512:640], grads[rows, 512:640])
        d = d * gain_t
        mean = jnp.sum(d, axis=0, keepdims=True) * (1.0 / C)
        along = jnp.sum(d * hat, axis=0, keepdims=True) * (1.0 / C)
        feature_gradient[:, rows] = inverse * (d - mean - hat * along) + cot[:, rows].astype(F32)
        layer_out[:, rows] = (x + nt(w_back[...], grads[rows, 512:768])).astype(BF16)
        return 0

    lax.fori_loop(0, PTS // chunk, part, 0, unroll=8)


def unpack_kernel(place, own, other, weights, gain_gradient, packed):
    mine = place[1]
    factor = (PTS * 256) ** (-0.5)
    packed[pl.ds(pl.multiple_of(mine * HALF, HALF), HALF), :] = own[...] * factor
    packed[pl.ds(pl.multiple_of((1 - mine) * HALF, HALF), HALF), :] = other[...] * factor
    for i, (tail, side) in enumerate(((960, 0), (768, 0), (768, 64))):
        weights[i, :, 0:128] = packed[192 * i:192 * (i + 1), :]
        weights[i, :, 128:C] = packed[tail:tail + 192, side:side + 64]
    weights[3, 0:128, :] = packed[576:768, :].T
    weights[3, 128:C, :] = packed[960:1152, :].T[64:128, :]
    gain_gradient[:, 0:128] = packed[1152:1153, :]
    gain_gradient[:, 128:C] = packed[1153:1154, 0:64]


def call(kernel, outs, specs, scratch=(), limit=24, micros=1.0, aliases=None):
    return pl.pallas_call(
        kernel,
        out_shape=[jax.ShapeDtypeStruct(s, t) for s, t in outs],
        in_specs=specs,
        out_specs=[ANY if i in (aliases or {}).values() else VMEM for i in range(len(outs))],
        input_output_aliases=aliases or {},
        scratch_shapes=[pltpu.VMEM(s, t) for s, t in scratch],
        cost_estimate=pl.CostEstimate(flops=int(micros * 1e9), bytes_accessed=int(micros * 3e6), transcendentals=0),
        compiler_params=pltpu.CompilerParams(vmem_limit_bytes=limit * 1024 * 1024),
    )


def neighbours(first, second, axes, count):
    pairs = [(i, i ^ 1) for i in range(count)]
    across = [(i, min(max(((i + 1) ^ 1) - 1, 0), count - 1)) for i in range(count)]
    return lax.ppermute(first, axes, pairs), lax.ppermute(second, axes, across)


def swapped(x):
    return lax.ppermute(x, "c", [(0, 1), (1, 0)])


def exchanged(x, axes):
    return lax.all_to_all(x, axes, 0, 0, tiled=True)


def local_prepare(after, points, gain, w_query, w_key, w_value, w_out, cotangent, picks):
    big = ((PAD, 128), F32)
    outs = [big] * 6 + [((C, PTS), BF16), ((C, 640), BF16), ((C, 256), BF16)]
    outs = outs + [((NWIN * WIN, NEAR), BF16), ((NEAR, NWIN * WIN), BF16)]
    return call(prepare_kernel, outs, [ANY] + [VMEM] * 9, limit=24, micros=5.0)(
        after, points, gain.reshape(1, C), w_query, w_key, w_value, w_out, cotangent,
        picks.reshape(1, NWIN * WIN), picks.reshape(NWIN * WIN, 1))


def local_order(place, own, first, second):
    return call(order_kernel, [((3 * SAMP, C), BF16)], [SMEM] + [VMEM] * 3, limit=6)(
        place, own, first, second)[0]


def local_attend(lengths, place, near, gain, w_in, projections, hots):
    big = ((PAD, 128), F32)
    near_out = ((NEAR, 2 * C), BF16)
    side = ((3, SAMP, 2 * C), BF16)
    return call(
        attend_kernel,
        [near_out, side, side, near_out, ((PTS, 6 * 128), BF16), ((NEAR, C), F32), ((NEAR, C), BF16)],
        [SMEM] * 2 + [VMEM] * 13,
        [((NEAR, C), BF16), near_out] + [((NWIN * WIN, 2 * C), BF16)] * 2 + [big] * 6,
        limit=26, micros=14.0,
    )(lengths, place, *near, gain.reshape(1, C), w_in, *projections, *hots)


def local_weights(points, cotangent, w_in, normed_t, grads, d_near, rest, near_hat, near_normed, place):
    return call(weights_kernel, [((HALF, 128), F32)] * 2, [VMEM] * 9 + [SMEM], [((ROWS, 128), F32)],
                limit=14, micros=3.0)(
        points, cotangent, w_in, normed_t, grads, d_near, rest, near_hat, near_normed, place)


def local_sides(place, d_near, got):
    side = ((SAMP, 2 * C), BF16)
    outs = [side, side, ((SAMP, 2 * C), F32)]
    return call(sides_kernel, outs, [SMEM] + [VMEM] * 3, [((3 * SAMP, 2 * C), F32)], limit=6)(
        place, d_near, *got)


def local_finish(points, gain, w_in, w_back, cotangent, grads, middle, upper, lower):
    outs = [((C, PTS), BF16), ((C, PTS), F32), ((8, 128), F32)]
    return call(finish_kernel, outs, [VMEM] * 9, [((SAMP, 2 * C), BF16)], limit=12, micros=4.0)(
        points, gain.reshape(1, C), w_in, w_back, cotangent, grads, middle, upper, lower)


def local_fold(after, parts, copies):
    outs = [((copies,) + parts.shape[1:], F32)]
    return call(fold_kernel, outs, [ANY, VMEM], limit=6)(after, parts)[0]


def local_unpack(place, own, other):
    return call(
        unpack_kernel, [((4, C, C), F32), ((1, C), F32)], [SMEM, VMEM, VMEM], [((ROWS, 128), F32)],
        limit=8, micros=1.0,
    )(place, own, other)


def body(points, gain, w_query, w_key, w_value, w_out, lengths, picks, cotangent):
    points = points[0, 0].T
    cotangent = cotangent[0, 0].T
    lengths = lengths.reshape(NWIN)
    sample = call(sample_kernel, [((SAMP, C), BF16)], [VMEM], limit=6)(points)[0]
    place = jnp.stack([lax.axis_index("xl"), lax.axis_index("c")]).astype(jnp.int32)
    across = local_order(place, sample, *neighbours(sample, sample, GY, 4))
    near = (across,) + neighbours(across, across, GX, 64)
    *projections, normed_t, w_in, w_back, onehot, onehot_t = local_prepare(
        across, points, gain, w_query, w_key, w_value, w_out, cotangent, picks)
    hots = (onehot, onehot_t)
    d_near, d_first, d_second, rest, grads, near_hat, near_normed = local_attend(
        lengths, place, near, gain, w_in, projections, hots)
    got = neighbours(d_first, d_second, GY, 4)
    keep, send = local_weights(
        points, cotangent, w_in, normed_t, grads, d_near, rest, near_hat, near_normed, place)
    mixed = exchanged((keep + swapped(send)).reshape(16, HALF // 16, 128), XY)
    mixed = exchanged(local_fold(got[0], mixed, 8), "z")
    first, second, middle = local_sides(place, d_near, got)
    got = neighbours(first, second, GX, 64)
    own = exchanged(local_fold(got[0], mixed, 16), XY).reshape(HALF, 128)
    layer_out, feature_gradient, token = local_finish(
        points, gain, w_in, w_back, cotangent, grads, middle, *got)
    weights, gain_gradient = local_unpack(place, own, swapped(own))
    return layer_out.T[None, None], feature_gradient.T[None, None], weights, gain_gradient.reshape(C)


def solution(mesh):
    inner = Mesh(mesh.devices.reshape(8, 4, 2, 2, 2), ("z", "y", "xl", "xh", "c"))
    return jax.shard_map(
        body,
        mesh=inner,
        in_specs=(P(GX, GY, None, None), P(), P(), P(), P(), P(), P(GX, GY, None),
                  P(GX, GY, None, None), P(GX, GY, None, None)),
        out_specs=(P(GX, GY, None, None), P(GX, GY, None, None), P(), P()),
        check_vma=False,
    )
```

```python
import jax
import jax.numpy as jnp
from jax import lax
from jax.experimental import pallas as pl
from jax.experimental.pallas import tpu as pltpu
from jax.sharding import Mesh, PartitionSpec as P

C = 192
H = 6
DEPTH = 32
PTS = 1024
WIN = 64
NWIN = 24
SAMP = 64
NEAR = 9 * SAMP
PAD = PTS + WIN
ROWS = 1280
HALF = ROWS // 2
GX = ("z", "y", "xl")
GY = ("xh", "c")
XY = ("y", "xl", "xh")
SCALE = DEPTH ** (-0.5)
LOG2E = 1.4426950408889634
F32 = jnp.float32
BF16 = jnp.bfloat16
VMEM = pl.BlockSpec(memory_space=pltpu.VMEM)
SMEM = pl.BlockSpec(memory_space=pltpu.SMEM)
ANY = pl.BlockSpec(memory_space=pl.ANY)
TOGETHER = 6


def nn(a, b):
    return lax.dot_general(a, b, (((1,), (0,)), ((), ())), preferred_element_type=F32)


def nt(a, b):
    return lax.dot_general(a, b, (((1,), (1,)), ((), ())), preferred_element_type=F32)


def tn(a, b):
    return lax.dot_general(a, b, (((0,), (0,)), ((), ())), preferred_element_type=F32)


def standardize(x, axis):
    mean = jnp.sum(x, axis=axis, keepdims=True) * (1.0 / C)
    centred = x - mean
    variance = jnp.sum(centred * centred, axis=axis, keepdims=True) * (1.0 / C)
    inverse = lax.rsqrt(variance + 1e-05)
    return centred * inverse, inverse


def sample_kernel(points, sample):
    row = lax.broadcasted_iota(jnp.int32, (SAMP, PTS), 0) * 16
    column = lax.broadcasted_iota(jnp.int32, (SAMP, PTS), 1)
    sample[...] = nt(jnp.where(row == column, 1.0, 0.0).astype(BF16), points[...]).astype(BF16)


def gain_column(gain):
    return jnp.broadcast_to(gain[...], (128, C)).T


def order_kernel(place, own, first, second, across):
    odd = place[1]
    across[SAMP:2 * SAMP, :] = own[...]
    across[pl.ds(pl.multiple_of(2 * SAMP * (1 - odd), SAMP), SAMP), :] = first[...]
    across[pl.ds(pl.multiple_of(2 * SAMP * odd, SAMP), SAMP), :] = second[...]


def prepare_kernel(after, points, gain, wq, wk, wv, wo, cot, picks_row, picks_col,
                   qa, ka, va, da, kvb, qdb, normed_t, w_in, w_back, onehot, onehot_t):
    chunk = 128
    gain_t = gain_column(gain)
    empty = jnp.zeros((C, 64), BF16)
    back = wo[...].astype(F32).T.astype(BF16)
    w_in[:, 0:128] = wq[:, 0:128]
    w_in[:, 128:256] = wk[:, 0:128]
    w_in[:, 256:384] = wv[:, 0:128]
    w_in[:, 384:512] = jnp.concatenate([wk[:, 128:], wv[:, 128:]], axis=1)
    w_in[:, 512:640] = jnp.concatenate([wq[:, 128:], empty], axis=1)
    w_back[:, 0:128] = jnp.concatenate([empty, back[:, 128:]], axis=1)
    w_back[:, 128:256] = back[:, 0:128]

    def project(i, _):
        rows = pl.ds(pl.multiple_of(i * chunk, chunk), chunk)
        hat, _inv = standardize(points[:, rows].astype(F32), 0)
        normed = (hat * gain_t).astype(BF16)
        normed_t[:, rows] = normed
        wide = tn(normed, w_in[...])
        back = tn(cot[:, rows], w_back[...])
        for ref, x in ((qa, wide[:, :128]), (ka, wide[:, 128:256]), (va, wide[:, 256:384]),
                       (kvb, wide[:, 384:512]), (da, back[:, 128:]), (qdb, wide[:, 512:] + back[:, :128])):
            ref[rows, :] = x.astype(BF16).astype(F32)
        return 0

    lax.fori_loop(0, PTS // chunk, project, 0, unroll=8)
    zeros = jnp.zeros((WIN, 128), F32)
    for ref in (qa, ka, va, da, kvb, qdb):
        ref[PTS:, :] = zeros

    def rows_hot(i, _):
        rows = pl.ds(pl.multiple_of(i * WIN, WIN), WIN)
        ids = lax.broadcasted_iota(jnp.int32, (WIN, NEAR), 1)
        onehot[rows, :] = jnp.where(picks_col[rows, :] == ids, 1.0, 0.0).astype(BF16)
        return 0

    lax.fori_loop(0, NWIN, rows_hot, 0, unroll=12)

    def columns_hot(i, _):
        rows = pl.ds(pl.multiple_of(i * SAMP, SAMP), SAMP)
        ids = lax.broadcasted_iota(jnp.int32, (SAMP, NWIN * WIN), 0) + i * SAMP
        onehot_t[rows, :] = jnp.where(picks_row[...] == ids, 1.0, 0.0).astype(BF16)
        return 0

    lax.fori_loop(0, 9, columns_hot, 0, unroll=9)


def attend_kernel(lengths, place, own_near, first, second, gain, w_in, qa, ka, va, da, kvb, qdb, onehot, onehot_t,
                  d_near, d_first, d_second, rest, grads, near_hat, near_normed,
                  near_points, near_kv, pick, d_pick, oa_s, dqa_s, dka_s, dva_s, dkvb_s, dqob_s):
    odd = place[0]
    strip = 3 * SAMP
    near_points[strip:2 * strip, :] = own_near[...]
    near_points[pl.ds(pl.multiple_of(2 * strip * (1 - odd), SAMP), strip), :] = first[...]
    near_points[pl.ds(pl.multiple_of(2 * strip * odd, SAMP), strip), :] = second[...]
    hat, _inv = standardize(near_points[...].astype(F32), 1)
    near_hat[...] = hat
    normed = (hat * gain[...]).astype(BF16)
    near_normed[...] = normed
    near_kv[...] = nn(normed, w_in[:, 128:512]).astype(BF16)

    def choose(group):
        size = TOGETHER * WIN
        rows = pl.ds(pl.multiple_of(group * size, size), size)
        pick[rows, :] = nn(onehot[rows, :], near_kv[...]).astype(BF16)

    choose(0)

    lane_head = lax.broadcasted_iota(jnp.int32, (1, 128), 1) // DEPTH
    lanes = [jnp.where(lane_head == h, 1.0, 0.0).astype(BF16) for h in range(4)]
    key_id = lax.broadcasted_iota(jnp.int32, (1, 128), 1)
    slot = lax.broadcasted_iota(jnp.int32, (WIN, 1), 0)
    half_scale = jnp.where(key_id < 64, SCALE, 1.0)

    def per_head(x):
        return jnp.concatenate([x * lane for lane in lanes], axis=0)

    def down(parts):
        return jnp.concatenate(parts, axis=0)

    ones = jnp.ones((256, 128), BF16)

    def row_sum(x):
        high = x.astype(BF16)
        low = (x - high.astype(F32)).astype(BF16)
        return nn(jnp.concatenate([high, low], axis=1), ones)

    def softmax(scores, bias):
        scores = scores + bias
        top = jnp.max(scores, axis=-1, keepdims=True)
        weights = jnp.exp2((scores - top) * (SCALE * LOG2E))
        return weights * (1.0 / jnp.sum(weights, axis=-1, keepdims=True))

    def score_gradient(probs, d_probs):
        d_probs = d_probs.astype(BF16).astype(F32)
        inner = row_sum(d_probs * probs)
        return (probs * (d_probs - inner)).astype(BF16)

    def cut(x):
        return [x[WIN * h:WIN * (h + 1)] for h in range(4)]

    def merge(x):
        parts = [part * lane for part, lane in zip(cut(x), lanes32)]
        return (parts[0] + parts[1]) + (parts[2] + parts[3])

    lanes32 = [lane.astype(F32) for lane in lanes]

    def load(w, offset):
        count = lengths[w]
        rows = pl.ds(offset, WIN)
        own = pl.ds(pl.multiple_of(w * WIN, WIN), WIN)
        bias = jnp.where((key_id >= count) & (key_id < WIN), -1e30, 0.0)
        alive = slot < count
        keys = down([ka[rows, :].astype(BF16), pick[own, 0:128]])
        values = down([va[rows, :].astype(BF16), pick[own, 128:256]])
        both = down([kvb[rows, :].astype(BF16), pick[own, 256:384]])
        qe = per_head(qa[rows, :].astype(BF16))
        de = per_head(jnp.where(alive, da[rows, :], 0.0).astype(BF16))
        qde = per_head(jnp.where(alive, qdb[rows, :], 0.0).astype(BF16))
        return rows, own, bias, keys, values, both, qe, de, qde

    def scored(item):
        _, _, _, keys, values, both, qe, de, qde = item
        return nt(qe, keys), nt(de, values), nt(qde, both)

    def weighed(item, found):
        bias = item[2]
        scores, d_probs, mixed = [cut(x) for x in found]
        probs = [softmax(x, bias) for x in scores]
        probs_b = [softmax(x, bias) for x in mixed[:2]]
        d_scores = [score_gradient(p, x) for p, x in zip(probs, d_probs)]
        back = [score_gradient(p, x) for p, x in zip(probs_b, mixed[2:])]
        back = back + [p.astype(BF16) for p in probs_b]
        return down([p.astype(BF16) for p in probs]), down(d_scores), down(back)

    def stored(item, found):
        rows, own, _, keys, values, both, qe, de, qde = item
        probs, d_scores, back = found
        oa_s[rows, :] = merge(nn(probs, values))
        dqa_s[rows, :] = merge(nn(d_scores, keys)) * SCALE
        dqob_s[rows, :] = merge(nn(back, both)) * half_scale
        d_keys = tn(d_scores, qe) * SCALE
        d_values = tn(probs, de)
        d_both = tn(back, qde) * half_scale
        dka_s[rows, :] = d_keys[:WIN]
        dva_s[rows, :] = d_values[:WIN]
        dkvb_s[rows, :] = d_both[:WIN]
        d_pick[own, 0:128] = d_keys[WIN:].astype(BF16)
        d_pick[own, 128:256] = d_values[WIN:].astype(BF16)
        d_pick[own, 256:384] = d_both[WIN:].astype(BF16)

    def windows(group, offset):
        items = []
        for j in range(TOGETHER):
            items.append(load(group * TOGETHER + j, offset))
            offset = offset + lengths[group * TOGETHER + j]
        found = [scored(item) for item in items]
        choose(lax.rem(group + 1, NWIN // TOGETHER))
        found = [weighed(item, x) for item, x in zip(items, found)]
        for item, x in zip(items, found):
            stored(item, x)
        return offset

    lax.fori_loop(0, NWIN // TOGETHER, windows, jnp.int32(0))

    near = nn(onehot_t[...], d_pick[...])
    near16 = near.astype(BF16)
    d_near[...] = near16
    side = place[1]
    for i in range(3):
        d_first[i] = d_near[pl.ds(pl.multiple_of(192 * i + 128 * (1 - side), SAMP), SAMP), :]
        d_second[i] = d_near[pl.ds(pl.multiple_of(192 * i + 128 * side, SAMP), SAMP), :]
    rest[...] = (near - near16.astype(F32)).astype(BF16)
    for i, ref in enumerate((dqa_s, dka_s, dva_s, dkvb_s, dqob_s, oa_s)):
        grads[:, 128 * i:128 * (i + 1)] = ref[:PTS, :].astype(BF16)


def weights_kernel(points, cot, w_in, normed_t, grads, d_near, rest, near_hat, near_normed, place,
                   keep, send, packed):
    wide = nn(normed_t[...], grads[:, 0:640])
    out = nn(cot[...], grads[:, 512:768])
    near_wide = tn(near_normed[...], jnp.concatenate([d_near[...], rest[...]], axis=1))
    near_wide = near_wide[:, 0:384] + near_wide[:, 384:768]
    packed[0:192, :] = wide[:, 0:128]
    packed[192:384, :] = wide[:, 128:256] + near_wide[:, 0:128]
    packed[384:576, :] = wide[:, 256:384] + near_wide[:, 128:256]
    packed[576:768, :] = out[:, 128:256]
    packed[768:960, :] = wide[:, 384:512] + near_wide[:, 256:384]
    lane = lax.broadcasted_iota(jnp.int32, (C, 128), 1)
    packed[960:1152, :] = jnp.where(lane < 64, wide[:, 512:640], out[:, 0:128])

    def gain_part(i, total):
        rows = pl.ds(pl.multiple_of(i * 128, 128), 128)
        hat, _inv = standardize(points[:, rows].astype(F32), 0)
        return total + nt(w_in[...], grads[rows, 0:640]) * hat

    total = lax.fori_loop(0, PTS // 128, gain_part, jnp.zeros((C, 128), F32), unroll=8)
    w_kv = w_in[:, 128:512]
    d = nt(d_near[...], w_kv) + nt(rest[...], w_kv)
    near_total = jnp.sum((d * near_hat[...]).reshape(NEAR // 8, 8, C), axis=0)
    gains = jnp.sum(total.T, axis=0, keepdims=True) + jnp.sum(near_total, axis=0, keepdims=True)
    packed[1152:, :] = jnp.zeros((ROWS - 1152, 128), F32)
    packed[1152:1153, :] = gains[:, :128]
    packed[1153:1154, 0:64] = gains[:, 128:]
    mine = place[1]
    keep[...] = packed[pl.ds(pl.multiple_of(mine * HALF, HALF), HALF), :]
    send[...] = packed[pl.ds(pl.multiple_of((1 - mine) * HALF, HALF), HALF), :]


def sides_kernel(place, d_near, got, got_too, first, second, middle, sides):
    for i in range(3):
        own = d_near[192 * i + 64:192 * i + 128, :].astype(F32)
        sides[SAMP * i:SAMP * (i + 1), :] = own + got[i].astype(F32) + got_too[i].astype(F32)
    odd = place[0]
    first[...] = sides[pl.ds(pl.multiple_of(2 * SAMP * (1 - odd), SAMP), SAMP), :].astype(BF16)
    second[...] = sides[pl.ds(pl.multiple_of(2 * SAMP * odd, SAMP), SAMP), :].astype(BF16)
    middle[...] = sides[SAMP:2 * SAMP, :]


def fold_kernel(after, parts, out):
    total = parts[0]
    for i in range(1, parts.shape[0]):
        total = total + parts[i]
    for i in range(out.shape[0]):
        out[i] = total


def finish_kernel(points, gain, w_in, w_back, cot, grads, middle, upper, lower,
                  layer_out, feature_gradient, token, returned):
    token[...] = jnp.zeros(token.shape, F32)
    chunk = 128
    returned[...] = (middle[...] + upper[...].astype(F32) + lower[...].astype(F32)).astype(BF16)
    gain_t = gain_column(gain)

    def part(i, _):
        rows = pl.ds(pl.multiple_of(i * chunk, chunk), chunk)
        x = points[:, rows].astype(F32)
        hat, inverse = standardize(x, 0)
        row = lax.broadcasted_iota(jnp.int32, (chunk, SAMP), 0) + i * chunk
        column = lax.broadcasted_iota(jnp.int32, (chunk, SAMP), 1)
        spread = jnp.where(row == column * 16, 1.0, 0.0).astype(BF16)
        total = (grads[rows, 128:512].astype(F32) + nn(spread, returned[...])).astype(BF16)
        d = nt(w_in[:, 0:128], grads[rows, 0:128]) + nt(w_in[:, 128:512], total)
        d = d + nt(w_in[:, 512:640], grads[rows, 512:640])
        d = d * gain_t
        mean = jnp.sum(d, axis=0, keepdims=True) * (1.0 / C)
        along = jnp.sum(d * hat, axis=0, keepdims=True) * (1.0 / C)
        feature_gradient[:, rows] = inverse * (d - mean - hat * along) + cot[:, rows].astype(F32)
        layer_out[:, rows] = (x + nt(w_back[...], grads[rows, 512:768])).astype(BF16)
        return 0

    lax.fori_loop(0, PTS // chunk, part, 0, unroll=8)


def unpack_kernel(place, own, other, weights, gain_gradient):
    factor = (PTS * 256) ** (-0.5)

    def write(low, high):
        for i in range(3):
            weights[i, :, 0:128] = low[192 * i:192 * (i + 1), :] * factor
        weights[0, :, 128:C] = high[320:512, 0:64] * factor
        weights[1, :, 128:C] = high[128:320, 0:64] * factor
        weights[2, :, 128:C] = high[128:320, 64:128] * factor
        weights[3, 0:128, 0:64] = (low[576:640, :] * factor).T
        weights[3, 0:128, 64:C] = (high[0:128, :] * factor).T
        weights[3, 128:C, :] = (high[320:512, :] * factor).T[64:128, :]
        gain_gradient[:, 0:128] = high[512:513, :] * factor
        gain_gradient[:, 128:C] = high[513:514, 0:64] * factor

    @pl.when(place[1] == 0)
    def _():
        write(own, other)

    @pl.when(place[1] != 0)
    def _():
        write(other, own)


def call(kernel, outs, specs, scratch=(), limit=24, micros=1.0, aliases=None):
    return pl.pallas_call(
        kernel,
        out_shape=[jax.ShapeDtypeStruct(s, t) for s, t in outs],
        in_specs=specs,
        out_specs=[ANY if i in (aliases or {}).values() else VMEM for i in range(len(outs))],
        input_output_aliases=aliases or {},
        scratch_shapes=[pltpu.VMEM(s, t) for s, t in scratch],
        cost_estimate=pl.CostEstimate(flops=int(micros * 1e9), bytes_accessed=int(micros * 3e6), transcendentals=0),
        compiler_params=pltpu.CompilerParams(vmem_limit_bytes=limit * 1024 * 1024),
    )


def neighbours(first, second, axes, count):
    pairs = [(i, i ^ 1) for i in range(count)]
    across = [(i, min(max(((i + 1) ^ 1) - 1, 0), count - 1)) for i in range(count)]
    return lax.ppermute(first, axes, pairs), lax.ppermute(second, axes, across)


def swapped(x):
    return lax.ppermute(x, "c", [(0, 1), (1, 0)])


def exchanged(x, axes):
    return lax.all_to_all(x, axes, 0, 0, tiled=True)


def local_prepare(after, points, gain, w_query, w_key, w_value, w_out, cotangent, picks):
    big = ((PAD, 128), F32)
    outs = [big] * 6 + [((C, PTS), BF16), ((C, 640), BF16), ((C, 256), BF16)]
    outs = outs + [((NWIN * WIN, NEAR), BF16), ((NEAR, NWIN * WIN), BF16)]
    return call(prepare_kernel, outs, [ANY] + [VMEM] * 9, limit=24, micros=5.0)(
        after, points, gain.reshape(1, C), w_query, w_key, w_value, w_out, cotangent,
        picks.reshape(1, NWIN * WIN), picks.reshape(NWIN * WIN, 1))


def local_order(place, own, first, second):
    return call(order_kernel, [((3 * SAMP, C), BF16)], [SMEM] + [VMEM] * 3, limit=6)(
        place, own, first, second)[0]


def local_attend(lengths, place, near, gain, w_in, projections, hots):
    big = ((PAD, 128), F32)
    near_out = ((NEAR, 2 * C), BF16)
    side = ((3, SAMP, 2 * C), BF16)
    return call(
        attend_kernel,
        [near_out, side, side, near_out, ((PTS, 6 * 128), BF16), ((NEAR, C), F32), ((NEAR, C), BF16)],
        [SMEM] * 2 + [VMEM] * 13,
        [((NEAR, C), BF16), near_out] + [((NWIN * WIN, 2 * C), BF16)] * 2 + [big] * 6,
        limit=26, micros=14.0,
    )(lengths, place, *near, gain.reshape(1, C), w_in, *projections, *hots)


def local_weights(points, cotangent, w_in, normed_t, grads, d_near, rest, near_hat, near_normed, place):
    return call(weights_kernel, [((HALF, 128), F32)] * 2, [VMEM] * 9 + [SMEM], [((ROWS, 128), F32)],
                limit=14, micros=3.0)(
        points, cotangent, w_in, normed_t, grads, d_near, rest, near_hat, near_normed, place)


def local_sides(place, d_near, got):
    side = ((SAMP, 2 * C), BF16)
    outs = [side, side, ((SAMP, 2 * C), F32)]
    return call(sides_kernel, outs, [SMEM] + [VMEM] * 3, [((3 * SAMP, 2 * C), F32)], limit=6)(
        place, d_near, *got)


def local_finish(points, gain, w_in, w_back, cotangent, grads, middle, upper, lower):
    outs = [((C, PTS), BF16), ((C, PTS), F32), ((8, 128), F32)]
    return call(finish_kernel, outs, [VMEM] * 9, [((SAMP, 2 * C), BF16)], limit=12, micros=4.0)(
        points, gain.reshape(1, C), w_in, w_back, cotangent, grads, middle, upper, lower)


def local_fold(after, parts, copies):
    outs = [((copies,) + parts.shape[1:], F32)]
    return call(fold_kernel, outs, [ANY, VMEM], limit=6)(after, parts)[0]


def local_unpack(place, own, other):
    return call(
        unpack_kernel, [((4, C, C), F32), ((1, C), F32)], [SMEM, VMEM, VMEM],
        limit=8, micros=1.0,
    )(place, own, other)


def body(points, gain, w_query, w_key, w_value, w_out, lengths, picks, cotangent):
    points = points[0, 0].T
    cotangent = cotangent[0, 0].T
    lengths = lengths.reshape(NWIN)
    sample = call(sample_kernel, [((SAMP, C), BF16)], [VMEM], limit=6)(points)[0]
    place = jnp.stack([lax.axis_index("xl"), lax.axis_index("c")]).astype(jnp.int32)
    across = local_order(place, sample, *neighbours(sample, sample, GY, 4))
    near = (across,) + neighbours(across, across, GX, 64)
    *projections, normed_t, w_in, w_back, onehot, onehot_t = local_prepare(
        across, points, gain, w_query, w_key, w_value, w_out, cotangent, picks)
    hots = (onehot, onehot_t)
    d_near, d_first, d_second, rest, grads, near_hat, near_normed = local_attend(
        lengths, place, near, gain, w_in, projections, hots)
    got = neighbours(d_first, d_second, GY, 4)
    keep, send = local_weights(
        points, cotangent, w_in, normed_t, grads, d_near, rest, near_hat, near_normed, place)
    mixed = exchanged((keep + swapped(send)).reshape(16, HALF // 16, 128), XY)
    mixed = exchanged(local_fold(got[0], mixed, 8), "z")
    first, second, middle = local_sides(place, d_near, got)
    got = neighbours(first, second, GX, 64)
    own = exchanged(local_fold(got[0], mixed, 16), XY).reshape(HALF, 128)
    layer_out, feature_gradient, token = local_finish(
        points, gain, w_in, w_back, cotangent, grads, middle, *got)
    weights, gain_gradient = local_unpack(place, own, swapped(own))
    return layer_out.T[None, None], feature_gradient.T[None, None], weights, gain_gradient.reshape(C)


def solution(mesh):
    inner = Mesh(mesh.devices.reshape(8, 4, 2, 2, 2), ("z", "y", "xl", "xh", "c"))
    return jax.shard_map(
        body,
        mesh=inner,
        in_specs=(P(GX, GY, None, None), P(), P(), P(), P(), P(), P(GX, GY, None),
                  P(GX, GY, None, None), P(GX, GY, None, None)),
        out_specs=(P(GX, GY, None, None), P(GX, GY, None, None), P(), P()),
        check_vma=False,
    )
```
